256 devices in a mesh: patch: 64 (over x_lo, z, y), head: 4 (over x_hi, core).
Axes of the slice: x: 4 (x_hi: 2, x_lo: 2; x = x_hi * 2 + x_lo), y: 4, z: 8, core: 2. Of those that a mesh axis runs over, the one named last changes fastest.
Arguments:
- tokens: bfloat16 [12288, 3072], P('patch'), may hold values from -6 to 6
- valid_counts: int32 [64], replicated, may hold values from 96 to 192, as said below
- mod_shift: float32 [3072], replicated, may hold values from -3 to 3
- mod_scale: float32 [3072], replicated, may hold values from -3 to 3
- mod_gate: float32 [3072], P('head'), may hold values from 8 to 64
- q_gain: float32 [128], replicated, may hold values from 0.6 to 96
- w_qkv: bfloat16 [3072, 3, 1536], P('patch', None, 'head'), may hold values from -0.109375 to 0.109375
- w_out: bfloat16 [1536, 3072], P('head', 'patch'), may hold values from -0.15625 to 0.15625
- stale_keys: bfloat16 [12288, 1536], P('patch', 'head'), may hold values from -8 to 8
- stale_values: bfloat16 [12288, 1536], P('patch', 'head'), may hold values from -6 to 6
Outputs:
- mixed: bfloat16 [12288, 3072], P('patch', 'head')
The draws below stay inside these ranges and needn't reach their ends.
Inputs may be any that keep to these rules, and one draw needn't show every extreme that they name: `valid_counts`: every slab has at least half of its slots real; some slab is full in every draw.
All inputs are finite; a program needn't handle non-finite values.
Results may differ from the reference program's by a relative error of at most 0.019.
Values may be sent and summed in bfloat16 or wider, within the bound.
A program may use at most 128 MiB of HBM per device.

```python
import math
import jax
import jax.numpy as jnp
from jax import lax

D = 3072
HEADS = 12
HEAD_DIM = 128
TOK_DEV = 192
HQ = 1536
SLABS = 64
PATCHES = 12288


def draw_valid_counts(key, part):
    key = jax.random.fold_in(key, 11)
    counts = jax.random.randint(key, (SLABS,), TOK_DEV // 2, TOK_DEV + 1)
    chosen = jax.random.randint(jax.random.fold_in(key, 5), (), 0, SLABS)
    return counts.at[chosen].set(TOK_DEV).astype(jnp.int32)


def draw_q_gain(key, part):
    key = jax.random.fold_in(key, 23)
    gains = jax.random.uniform(key, (HEAD_DIM,), jnp.float32, 0.6, 1.6)
    return gains.astype(jnp.float32)


def draw_stale_keys(key, part):
    key = jax.random.fold_in(key, 29)
    base = jnp.clip(jax.random.normal(key, (PATCHES, HQ), jnp.float32), -6.0, 6.0)
    return base.astype(jnp.bfloat16)


def block_scale(own_key, dims, pieces, smallest, largest):
    def one(position, shards_of):
        steps = jax.random.uniform(jax.random.fold_in(jax.random.fold_in(own_key, 6), position), (shards_of,), jnp.float32, smallest / len(pieces), largest / len(pieces))
        return jnp.repeat(jnp.exp(steps), dims[position] // shards_of).reshape((-1,) + (1,) * (len(dims) - position - 1))

    level = one(*pieces[0])
    for cut in pieces[1:]:
        level = level * one(*cut)
    return level


def normal_values(own_key, extent, spread, bound, pieces=(), held_as=jnp.bfloat16):
    factor_of = block_scale(own_key, extent, pieces, -0.22, 0.18) if pieces else 1.0
    result = jax.random.normal(own_key, extent, jnp.float32) * spread * factor_of
    return jnp.minimum(jnp.maximum(result, -bound), bound).astype(held_as)


def setup_inputs(seed: int = 0) -> dict:
    splits = jax.random.split(jax.random.key(seed), 11)
    tokens = normal_values(splits[0], (PATCHES, D), 1.0, 6.0, ((0, 64),))
    valid_counts = draw_valid_counts(jax.random.fold_in(splits[10], 71), 0)
    mod_shift = normal_values(splits[2], (D,), 0.5, 3.0, (), jnp.float32)
    mod_scale = normal_values(splits[3], (D,), 0.5, 3.0, (), jnp.float32)
    mod_gate = jnp.clip(jnp.exp(math.log(64.0) - 2.0794415 * jax.random.uniform(splits[4], (D,), jnp.float32) ** block_scale(splits[4], (D,), ((0, 4),), -0.2, 0.2)), 8.0, 64.0)
    q_gain = draw_q_gain(jax.random.fold_in(splits[10], 71), 0)
    w_qkv = normal_values(splits[6], (D, 3, HQ), D ** -0.5, 0.109375, ((0, 64), (2, 4)))
    w_out = normal_values(splits[7], (HQ, D), HQ ** -0.5, 0.15625, ((0, 4), (1, 64)))
    stale_keys = draw_stale_keys(jax.random.fold_in(splits[10], 71), 0)
    stale_values = normal_values(splits[9], (PATCHES, HQ), 1.0, 6.0, ((0, 64), (1, 4)))
    return {"tokens": tokens, "valid_counts": valid_counts, "mod_shift": mod_shift, "mod_scale": mod_scale, "mod_gate": mod_gate, "q_gain": q_gain, "w_qkv": w_qkv, "w_out": w_out, "stale_keys": stale_keys, "stale_values": stale_values}


def head_norm(raw):
    return raw / jnp.sqrt(lax.optimization_barrier(jnp.mean(raw * raw, axis=-1, keepdims=True)) + 1e-06)

def reference(tokens, valid_counts, mod_shift, mod_scale, mod_gate, q_gain, w_qkv, w_out, stale_keys, stale_values):
    values_f = tokens.astype(jnp.float32)
    mean = lax.optimization_barrier(jnp.mean(values_f, axis=1, keepdims=True))
    centred = values_f - mean
    variance = lax.optimization_barrier(jnp.mean(centred * centred, axis=1, keepdims=True))
    normed = centred / jnp.sqrt(variance + 1e-06)
    modulated = (normed * (1.0 + mod_scale) + mod_shift).astype(jnp.bfloat16)
    qkv = jnp.dot(modulated, w_qkv.reshape(D, 3 * HQ), preferred_element_type=jnp.float32)
    raw_queries = qkv[:, :HQ].reshape(PATCHES, HEADS, HEAD_DIM)
    raw_keys = qkv[:, HQ:2 * HQ].reshape(PATCHES, HEADS, HEAD_DIM)
    queries = (head_norm(raw_queries) * q_gain).astype(jnp.bfloat16).reshape(PATCHES, HQ)
    fresh_keys = head_norm(raw_keys).astype(jnp.bfloat16).reshape(PATCHES, HQ)
    fresh_values = qkv[:, 2 * HQ:].astype(jnp.bfloat16)
    positions = jnp.arange(PATCHES, dtype=jnp.int32)
    valid = positions % TOK_DEV < valid_counts[positions // TOK_DEV]
    score_scale = 1.0 / HEAD_DIM ** 0.5

    def one_slab(slab):
        first = (slab * TOK_DEV).astype(jnp.int32)
        zero = jnp.zeros((), jnp.int32)
        slab_queries = lax.dynamic_slice(queries, (first, zero), (TOK_DEV, HQ))
        own_keys = lax.dynamic_slice(fresh_keys, (first, zero), (TOK_DEV, HQ))
        own_values = lax.dynamic_slice(fresh_values, (first, zero), (TOK_DEV, HQ))
        key_rows = lax.dynamic_update_slice(stale_keys, own_keys, (first, zero))
        value_rows = lax.dynamic_update_slice(stale_values, own_values, (first, zero))
        qh = slab_queries.astype(jnp.float32).reshape(TOK_DEV, HEADS, HEAD_DIM)
        kh = key_rows.astype(jnp.float32).reshape(PATCHES, HEADS, HEAD_DIM)
        vh = value_rows.astype(jnp.float32).reshape(PATCHES, HEADS, HEAD_DIM)
        scores = jnp.einsum('qhd,khd->hqk', qh, kh) * score_scale
        scores = jnp.where(valid[None, None, :], scores, -jnp.inf)
        rowmax = lax.optimization_barrier(jnp.max(scores, axis=2, keepdims=True))
        weights = jnp.exp(scores - rowmax)
        total = lax.optimization_barrier(jnp.sum(weights, axis=2))
        rounded = weights.astype(jnp.bfloat16).astype(jnp.float32)
        numer = jnp.einsum('hqk,khd->hqd', rounded, vh)
        attended = numer / total[:, :, None]
        return jnp.transpose(attended, (1, 0, 2)).reshape(TOK_DEV, HQ).astype(jnp.bfloat16)
    attended = lax.map(one_slab, jnp.arange(SLABS, dtype=jnp.int32)).reshape(PATCHES, HQ)
    projected = jnp.dot(attended, w_out, preferred_element_type=jnp.float32)
    return (mod_gate * projected).astype(jnp.bfloat16)
```

```python
import functools
import math

import jax
import jax.numpy as jnp
from jax import lax
from jax.experimental import pallas as pl
from jax.experimental.pallas import tpu as pltpu
from jax.sharding import PartitionSpec as P

MESH = pl.DeviceIdType.MESH
F32 = jnp.float32
BF16 = jnp.bfloat16
ROWS = 192
D = 3072
HQ = 384
HD = 128
NZ, NY, NX = 8, 4, 4
SHARD = 48
C2 = math.log2(math.e) / math.sqrt(HD)
NEG = -1e30
N_SEM = 104


def dev(x, z, y, c):
    return ((lax.rem(x, 2) * NZ + z) * NY + y, (x // 2) * 2 + c)


def kernel(counts, tokens, scale, shift, gain, gate, w_in, wo_in, k_in, v_in, out,
           tok, xmod, wbuf, kv, mask, qbuf, s_scr, stat, osend, orecv, att, wo, gbuf, mix,
           ssem, rsem):
    p = lax.axis_index("patch")
    h = lax.axis_index("head")
    xl, z, y = p // (NZ * NY), lax.rem(p // NY, NZ), lax.rem(p, NY)
    xh, c = h // 2, lax.rem(h, 2)
    x = xh * 2 + xl
    oc = 1 - c

    def zat(k):
        return lax.rem(z + k + NZ, NZ)

    def yat(k):
        return lax.rem(y + k + NY, NY)

    def xat(k):
        return lax.rem(x + k + NX, NX)

    def to_z(k):
        return dev(x, zat(k), y, c)

    def to_y(k):
        return dev(x, z, yat(k), c)

    sibling = dev(x, z, y, oc)
    stays = c == xl

    next_sem = [0]

    def new_sem():
        next_sem[0] += 1
        return next_sem[0] - 1

    class Link:
        def __init__(self, src, dst, target, landing=None):
            n = new_sem()
            self.send = pltpu.make_async_remote_copy(
                src_ref=src, dst_ref=dst, send_sem=ssem.at[n], recv_sem=rsem.at[n],
                device_id=target, device_id_type=MESH)
            land = dst if landing is None else landing
            self.recv = pltpu.make_async_remote_copy(
                src_ref=land, dst_ref=land, send_sem=ssem.at[n], recv_sem=rsem.at[n],
                device_id=target, device_id_type=MESH)
            self.n = n
            self.sent = False

        def start(self):
            self.send.start()
            return self

        def arrived(self):
            self.recv.wait_recv()

        def done(self):
            if not self.sent:
                self.send.wait_send()
                self.sent = True

    links = []

    def post(src, dst, target, landing=None):
        link = Link(src, dst, target, landing).start()
        links.append(link)
        return link

    barrier = pltpu.get_barrier_semaphore()
    for k in range(NX):
        for cc in range(2):
            if k == 0 and cc == 0:
                continue
            pl.semaphore_signal(barrier, inc=1, device_id=dev(xat(k), z, y, lax.rem(c + cc, 2)),
                                device_id_type=MESH)
    for k in range(1, NZ):
        pl.semaphore_signal(barrier, inc=1, device_id=to_z(k), device_id_type=MESH)
    for k in range(1, NY):
        pl.semaphore_signal(barrier, inc=1, device_id=to_y(k), device_id_type=MESH)
    pl.semaphore_wait(barrier, 2 * NX - 1 + NZ - 1 + NY - 1)

    partner = dev(xh * 2 + c, z, y, xl)

    class Swap:
        def __init__(self, src, here, there):
            n = new_sem()
            self.local = pltpu.make_async_copy(src, here, ssem.at[n])
            self.remote = pltpu.make_async_remote_copy(
                src_ref=src, dst_ref=there, send_sem=ssem.at[n], recv_sem=rsem.at[n],
                device_id=partner, device_id_type=MESH)
            self.landing = pltpu.make_async_remote_copy(
                src_ref=here, dst_ref=here, send_sem=ssem.at[n], recv_sem=rsem.at[n],
                device_id=partner, device_id_type=MESH)

        def start(self):
            @pl.when(stays)
            def _():
                self.local.start()

            @pl.when(jnp.logical_not(stays))
            def _():
                self.remote.start()
            return self

        def wait(self):
            @pl.when(stays)
            def _():
                self.local.wait()

            @pl.when(jnp.logical_not(stays))
            def _():
                self.remote.wait_send()
                self.landing.wait_recv()

    in_q = Swap(w_in.at[pl.ds(0, 1)], wbuf.at[pl.ds(0, 1), c, z, y], wbuf.at[pl.ds(0, 1), oc, z, y]).start()
    in_kv = Swap(w_in.at[pl.ds(1, 2)], wbuf.at[pl.ds(1, 2), c, z, y], wbuf.at[pl.ds(1, 2), oc, z, y]).start()

    half = ROWS // 2
    tok_sem = [new_sem(), new_sem()]
    tok_local = pltpu.make_async_copy(tokens, tok, ssem.at[tok_sem[0]])

    def tok_copy(k):
        rows = pl.ds(k * half, half)
        xo = xat(1 - 2 * k)
        return pltpu.make_async_remote_copy(
            src_ref=tokens.at[rows], dst_ref=tok.at[rows], send_sem=ssem.at[tok_sem[k]],
            recv_sem=rsem.at[tok_sem[k]], device_id=dev(xo, z, y, oc), device_id_type=MESH)

    @pl.when(stays)
    def _():
        tok_local.start()

    @pl.when(jnp.logical_not(stays))
    def _():
        tok_copy(0).start()
        tok_copy(1).start()

    in_k = Swap(k_in, kv.at[0, c, z], kv.at[0, oc, z]).start()
    in_v = Swap(v_in, kv.at[1, c, z], kv.at[1, oc, z]).start()
    in_g = Swap(gate, gbuf, gbuf).start()

    zh = z // 4
    wo_x, wo_c = 2 * xl + zh, xh
    wo_self = jnp.logical_and(wo_x == x, wo_c == c)
    wo_sem = [new_sem(), new_sem()]

    def wo_first(core):
        return pltpu.make_async_remote_copy(
            src_ref=wo_in, dst_ref=wo.at[h, lax.rem(z, 4), y], send_sem=ssem.at[wo_sem[core]],
            recv_sem=rsem.at[wo_sem[core]], device_id=dev(wo_x, z, y, wo_c), device_id_type=MESH)

    def wo_local(core):
        return pltpu.make_async_copy(wo_in, wo.at[h, lax.rem(z, 4), y], ssem.at[wo_sem[core]])

    for core in range(2):
        @pl.when(jnp.logical_and(c == core, wo_self))
        def _():
            wo_local(core).start()

        @pl.when(jnp.logical_and(c == core, jnp.logical_not(wo_self)))
        def _():
            wo_first(core).start()

    in_q.wait()
    wq_z = []
    for k in (1, -1, 2, -2, 3, -3, 4):
        wq_z.append(post(wbuf.at[0, c, z, y], wbuf.at[0, c, z, y], to_z(k),
                         landing=wbuf.at[0, c, zat(-k), y]))
    in_kv.wait()

    def ring(block, first, second):
        state = {}

        def step(s):
            if s > 0:
                for link in state[s - 1]:
                    link.arrived()
            if s > 3:
                return
            if s < 3:
                right = post(block(zat(-s)), block(zat(-s)), to_z(1), landing=block(zat(-1 - s)))
                left = post(block(zat(s)), block(zat(s)), to_z(-1), landing=block(zat(1 + s)))
            else:
                right = post(first(zat(-s)), first(zat(-s)), to_z(1), landing=first(zat(-1 - s)))
                left = post(second(zat(s)), second(zat(s)), to_z(-1), landing=second(zat(1 + s)))
            state[s] = (right, left)
        return step

    wkv_step = ring(lambda b: wbuf.at[pl.ds(1, 2), c, b, y],
                    lambda b: wbuf.at[pl.ds(1, 1), c, b, y],
                    lambda b: wbuf.at[pl.ds(2, 1), c, b, y])
    kv_ring = ring(lambda b: kv.at[:, c, b],
                   lambda b: kv.at[pl.ds(0, 1), c, b],
                   lambda b: kv.at[pl.ds(1, 1), c, b])
    kv_sib = []

    def kv_share(b):
        kv_sib.append(post(kv.at[:, c, b], kv.at[:, c, b], sibling, landing=kv.at[:, oc, b]))

    def kv_step(s):
        kv_ring(s)
        if s == 0:
            kv_share(z)
        elif s < 4:
            kv_share(zat(-s))
            kv_share(zat(s))
        else:
            kv_share(zat(4))

    def w_y(i):
        st = {}
        sib = []

        def share(b):
            sib.append(post(wbuf.at[i, c, :, b], wbuf.at[i, c, :, b], sibling,
                            landing=wbuf.at[i, oc, :, b]))

        def begin():
            src = wbuf.at[i, c, :, y]
            st["r"] = post(src, src, to_y(1), landing=wbuf.at[i, c, :, yat(-1)])
            st["l"] = post(src, src, to_y(-1), landing=wbuf.at[i, c, :, yat(1)])
            share(y)

        def middle():
            lo, hi = pl.ds(0, 4), pl.ds(4, 4)
            st["r"].arrived()
            src = wbuf.at[i, c, lo, yat(-1)]
            st["rr"] = post(src, src, to_y(1), landing=wbuf.at[i, c, lo, yat(2)])
            st["l"].arrived()
            src = wbuf.at[i, c, hi, yat(1)]
            st["ll"] = post(src, src, to_y(-1), landing=wbuf.at[i, c, hi, yat(2)])
            share(yat(-1))
            share(yat(1))

        def end():
            st["rr"].arrived()
            st["ll"].arrived()
            share(yat(2))

        def ready():
            for link in sib:
                link.arrived()
        return begin, middle, end, ready

    q_begin, q_middle, q_end, q_ready = w_y(0)
    k_begin, k_middle, k_end, k_ready = w_y(1)
    v_begin, v_middle, v_end, v_ready = w_y(2)

    wkv_step(0)

    rows_i = lax.broadcasted_iota(jnp.int32, (ROWS, HD), 0)
    lanes_i = lax.broadcasted_iota(jnp.int32, (ROWS, HD), 1)
    for s in range(16):
        limit = counts[s * NY + y]
        keep = jnp.logical_or(rows_i < limit, lanes_i > 0)
        mask[s] = jnp.where(keep, 0.0, NEG).astype(BF16)

    wkv_step(1)
    for link in wq_z:
        link.arrived()
    q_begin()
    in_k.wait()
    in_v.wait()
    kv_step(0)
    wkv_step(2)

    @pl.when(stays)
    def _():
        tok_local.wait()

    @pl.when(jnp.logical_not(stays))
    def _():
        tok_copy(0).wait()
        tok_copy(1).wait()

    def modulate(i, carry):
        r = pl.ds(pl.multiple_of(i * 16, 16), 16)
        t = tok[r, :].astype(F32)
        mean = jnp.mean(t, axis=1, keepdims=True)
        t = t - mean
        var = jnp.mean(t * t, axis=1, keepdims=True)
        t = t * lax.rsqrt(var + 1e-6)
        xmod[r, :] = (t * (1.0 + scale[...]) + shift[...]).astype(BF16)
        return carry

    lax.fori_loop(0, ROWS // 16, modulate, 0)
    wkv_step(3)
    q_middle()
    wkv_step(4)
    kv_step(1)
    q_end()
    k_begin()
    q_ready()

    def project(i):
        return jnp.dot(xmod[...], wbuf[i].reshape(D, HQ), preferred_element_type=F32)

    def head_norm(r):
        return r / jnp.sqrt(jnp.mean(r * r, axis=1, keepdims=True) + 1e-6)

    raw = project(0)
    for j in range(3):
        cols = slice(j * HD, (j + 1) * HD)
        qbuf[y, :, cols] = (head_norm(raw[:, cols]) * gain[...]).astype(BF16)
    q_links = {}
    for d in (1, 3, 2):
        q_links[d] = post(qbuf.at[y], qbuf.at[y], to_y(d), landing=qbuf.at[yat(-d)])
    kv_step(2)
    k_middle()
    v_begin()

    holds = zh == xl
    wo_rows = pl.ds(2 * c, 2)
    for core in range(2):
        from_self = jnp.logical_and(wo_self, c == core)

        @pl.when(from_self)
        def _():
            wo_local(core).wait()

        @pl.when(jnp.logical_and(holds, jnp.logical_not(from_self)))
        def _():
            wo_first(core).wait_recv()

        @pl.when(jnp.logical_and(c == core, jnp.logical_not(wo_self)))
        def _():
            wo_first(core).wait_send()

    woz_sem = [new_sem() for _ in range(7)]

    def woz(k, n):
        blk = wo.at[wo_rows, lax.rem(z, 4), y]
        return pltpu.make_async_remote_copy(
            src_ref=blk, dst_ref=blk, send_sem=ssem.at[woz_sem[n]], recv_sem=rsem.at[woz_sem[n]],
            device_id=to_z(k), device_id_type=MESH)

    def woz_landing(k, n):
        blk = wo.at[wo_rows, lax.rem(zat(-k), 4), y]
        return pltpu.make_async_remote_copy(
            src_ref=blk, dst_ref=blk, send_sem=ssem.at[woz_sem[n]], recv_sem=rsem.at[woz_sem[n]],
            device_id=to_z(k), device_id_type=MESH)

    zks = (1, -1, 2, -2, 3, -3, 4)
    kv_step(3)

    @pl.when(holds)
    def _():
        for n, k in enumerate(zks):
            woz(k, n).start()

    kv_step(4)
    for link in kv_sib:
        link.arrived()

    ones = jnp.ones((768, HD), BF16)

    def attend(yq, j):
        cols = pl.ds(pl.multiple_of(j * HD, HD), HD)
        first = (lax.broadcasted_iota(jnp.int32, (ROWS, HD), 1) == 0)
        q = jnp.concatenate([qbuf[yq, :, cols], jnp.where(first, 1.0, 0.0).astype(BF16)], axis=1)
        top = None
        for b in range(4):
            cc, zz = b // 2, 4 * (b % 2)
            kb = kv[0, cc, zz:zz + 4, :, cols].reshape(768, HD)
            mb = mask[4 * b:4 * b + 4].reshape(768, HD)
            kb = jnp.concatenate([kb, mb], axis=1)
            s = lax.dot_general(q, kb, (((1,), (1,)), ((), ())), preferred_element_type=F32)
            s_scr[:, 768 * b:768 * (b + 1)] = s
            for t in range(6):
                piece = s[:, t * HD:(t + 1) * HD]
                top = piece if top is None else jnp.maximum(top, piece)
        m = jnp.max(top, axis=1, keepdims=True)
        acc = jnp.zeros((ROWS, 2 * HD), F32)
        for b in range(4):
            cc, zz = b // 2, 4 * (b % 2)
            w = jnp.exp2((s_scr[:, 768 * b:768 * (b + 1)] - m) * C2).astype(BF16)
            vb = jnp.concatenate([kv[1, cc, zz:zz + 4, :, cols].reshape(768, HD), ones], axis=1)
            acc = acc + jnp.dot(w, vb, preferred_element_type=F32)
        total = acc[:, HD:]
        o = acc[:, :HD] / total
        return o, m * C2 + jnp.log2(total)

    def partial(d):
        def one(j, carry):
            o, lse = attend(yat(d), j)
            osend[d, :, pl.ds(pl.multiple_of(j * HD, HD), HD)] = o.astype(BF16)
            lane = lax.broadcasted_iota(jnp.int32, (ROWS, HD), 1)
            stat[...] = jnp.where(lane % 4 == j, lse, stat[...])
            return carry

        stat[...] = jnp.zeros_like(stat)
        lax.fori_loop(0, 3, one, 0)
        lane = lax.broadcasted_iota(jnp.int32, (ROWS, HD), 1)
        full = stat[...]
        top = full.astype(BF16).astype(F32)
        mid = (full - top).astype(BF16).astype(F32)
        low = full - top - mid
        osend[d, :, HQ:] = jnp.where(lane < 4, top, jnp.where(lane < 8, mid, low)).astype(BF16)
        return post(osend.at[d], orecv.at[d], to_y(d), landing=orecv.at[d])

    o_links = []
    q_links[3].arrived()
    o_links.append(partial(1))
    k_end()
    v_middle()
    k_ready()
    raw = project(1)
    fresh_k = [head_norm(raw[:, j * HD:(j + 1) * HD]).astype(BF16) for j in range(3)]
    for j in range(3):
        mix[:, j * HD:(j + 1) * HD] = fresh_k[j]
    q_links[1].arrived()
    o_links.append(partial(3))
    v_end()

    for n, k in enumerate(zks):
        src_holds = (zat(-k) // 4) == xl

        @pl.when(src_holds)
        def _():
            woz_landing(k, n).wait_recv()

        @pl.when(holds)
        def _():
            woz(k, n).wait_send()
    blk = wo.at[wo_rows, :, y]
    wo_r = post(blk, blk, to_y(1), landing=wo.at[wo_rows, :, yat(-1)])
    wo_l = post(blk, blk, to_y(-1), landing=wo.at[wo_rows, :, yat(1)])
    v_ready()
    raw = project(2)
    mix[:, HQ:] = raw.astype(BF16)
    q_links[2].arrived()
    o_links.append(partial(2))

    wo_r.arrived()
    blk = wo.at[wo_rows, pl.ds(0, 2), yat(-1)]
    wo_rr = post(blk, blk, to_y(1), landing=wo.at[wo_rows, pl.ds(0, 2), yat(2)])
    wo_l.arrived()
    blk = wo.at[wo_rows, pl.ds(2, 2), yat(1)]
    wo_ll = post(blk, blk, to_y(-1), landing=wo.at[wo_rows, pl.ds(2, 2), yat(2)])

    for link in links:
        if link not in o_links and link is not wo_rr and link is not wo_ll:
            link.done()
    kv[0, c, z] = mix[:, :HQ]
    kv[1, c, z] = mix[:, HQ:]

    for link in o_links:
        link.arrived()
    att_links = []
    for j in range(3):
        cols = slice(j * HD, (j + 1) * HD)
        own, own_lse = attend(y, j)
        lane = lax.broadcasted_iota(jnp.int32, (ROWS, HD), 1)
        parts, lses = [own], [own_lse[:, :1]]
        for d in (1, 3, 2):
            parts.append(orecv[d, :, cols].astype(F32))
            st = jnp.where(jnp.logical_and(lane % 4 == j, lane < 12), orecv[d, :, HQ:].astype(F32), 0.0)
            lses.append(jnp.sum(st, axis=1, keepdims=True))
        top = functools.reduce(jnp.maximum, lses)
        ws = [jnp.exp2(v - top) for v in lses]
        total = functools.reduce(jnp.add, ws)
        mixd = functools.reduce(jnp.add, [w * o for w, o in zip(ws, parts)])
        att[x, :, cols] = (mixd / total).astype(BF16)
        for k in (1, 3, 2):
            att_links.append(post(att.at[x, :, pl.ds(j * HD, HD)], att.at[x, :, pl.ds(j * HD, HD)],
                                  dev(xat(k), z, y, c),
                                  landing=att.at[xat(-k), :, pl.ds(j * HD, HD)]))
    wo_rr.arrived()
    wo_ll.arrived()
    blk = wo.at[wo_rows]
    wo_s = post(blk, blk, sibling, landing=wo.at[pl.ds(2 * oc, 2)])
    wo_s.arrived()
    for link in att_links:
        link.arrived()
    in_g.wait()
    acc = jnp.zeros((ROWS, 768), F32)
    for g in range(NX):
        acc = acc + lax.dot_general(att[g], wo[g].reshape(768, HQ), (((1,), (1,)), ((), ())),
                                    preferred_element_type=F32)
    mix[...] = (acc * gbuf[...]).astype(BF16)
    last = Swap(mix, out, out).start()
    last.wait()
    for link in links:
        link.done()
    assert next_sem[0] <= N_SEM, next_sem[0]


def shards(tokens, valid_counts, mod_shift, mod_scale, mod_gate, q_gain, w_qkv, w_out,
           stale_keys, stale_values):
    vm = pl.BlockSpec(memory_space=pltpu.VMEM)
    hbm = pl.BlockSpec(memory_space=pl.ANY)
    return pl.pallas_call(
        kernel,
        out_shape=jax.ShapeDtypeStruct((ROWS, 768), BF16),
        in_specs=[pl.BlockSpec(memory_space=pltpu.SMEM), hbm, vm, vm, vm, hbm, hbm, hbm, hbm, hbm],
        out_specs=hbm,
        scratch_shapes=[
            pltpu.VMEM((ROWS, D), BF16),
            pltpu.VMEM((ROWS, D), BF16),
            pltpu.VMEM((3, 2, NZ, NY, SHARD, HQ), BF16),
            pltpu.VMEM((2, 2, NZ, ROWS, HQ), BF16),
            pltpu.VMEM((16, ROWS, HD), BF16),
            pltpu.VMEM((NY, ROWS, HQ), BF16),
            pltpu.VMEM((ROWS, 16 * ROWS), F32),
            pltpu.VMEM((ROWS, HD), F32),
            pltpu.VMEM((NY, ROWS, HQ + HD), BF16),
            pltpu.VMEM((NY, ROWS, HQ + HD), BF16),
            pltpu.VMEM((NX, ROWS, HQ), BF16),
            pltpu.VMEM((4, 4, NY, SHARD, HQ), BF16),
            pltpu.VMEM((1, 768), F32),
            pltpu.VMEM((ROWS, 768), BF16),
            pltpu.SemaphoreType.DMA((N_SEM,)),
            pltpu.SemaphoreType.DMA((N_SEM,)),
        ],
        compiler_params=pltpu.CompilerParams(
            collective_id=0, has_side_effects=True, vmem_limit_bytes=48 * 2**20),
    )(valid_counts, tokens, mod_scale.reshape(1, D), mod_shift.reshape(1, D),
      q_gain.reshape(1, HD), mod_gate.reshape(1, 768), jnp.transpose(w_qkv, (1, 0, 2)),
      jnp.transpose(w_out), stale_keys, stale_values)


def solution(mesh):
    in_specs = (
        P("patch", None), P(), P(), P(), P("head"), P(), P("patch", None, "head"),
        P("head", "patch"), P("patch", "head"), P("patch", "head"),
    )
    return jax.shard_map(shards, mesh=mesh, in_specs=in_specs, out_specs=P("patch", "head"),
                         check_vma=False)
```

```python
import functools
import math

import jax
import jax.numpy as jnp
from jax import lax
from jax.experimental import pallas as pl
from jax.experimental.pallas import tpu as pltpu
from jax.sharding import PartitionSpec as P

MESH = pl.DeviceIdType.MESH
F32 = jnp.float32
BF16 = jnp.bfloat16
ROWS = 192
D = 3072
HQ = 384
HD = 128
NZ, NY, NX = 8, 4, 4
SHARD = 48
C2 = math.log2(math.e) / math.sqrt(HD)
NEG = -1e30
N_SEM = 112


def dev(x, z, y, c):
    return ((lax.rem(x, 2) * NZ + z) * NY + y, (x // 2) * 2 + c)


def kernel(counts, tokens, scale_in, shift_in, gain_in, gate, w_in, wo_in, k_in, v_in, out,
           tok, scale, shift, gain, xmod, wbuf, kv, mask, qbuf, stat, osend, orecv, att, wo, gbuf, mix,
           run_m, run_acc, ssem, rsem):
    p = lax.axis_index("patch")
    h = lax.axis_index("head")
    xl, z, y = p // (NZ * NY), lax.rem(p // NY, NZ), lax.rem(p, NY)
    xh, c = h // 2, lax.rem(h, 2)
    x = xh * 2 + xl
    oc = 1 - c

    def zat(k):
        return lax.rem(z + k + NZ, NZ)

    def yat(k):
        return lax.rem(y + k + NY, NY)

    def xat(k):
        return lax.rem(x + k + NX, NX)

    def to_z(k):
        return dev(x, zat(k), y, c)

    def to_y(k):
        return dev(x, z, yat(k), c)

    sibling = dev(x, z, y, oc)
    stays = c == xl

    next_sem = [0]

    def new_sem():
        next_sem[0] += 1
        return next_sem[0] - 1

    class Link:
        def __init__(self, src, dst, target, landing=None):
            n = new_sem()
            self.send = pltpu.make_async_remote_copy(
                src_ref=src, dst_ref=dst, send_sem=ssem.at[n], recv_sem=rsem.at[n],
                device_id=target, device_id_type=MESH)
            land = dst if landing is None else landing
            self.recv = pltpu.make_async_remote_copy(
                src_ref=land, dst_ref=land, send_sem=ssem.at[n], recv_sem=rsem.at[n],
                device_id=target, device_id_type=MESH)
            self.n = n
            self.sent = False

        def start(self):
            self.send.start()
            return self

        def arrived(self):
            self.recv.wait_recv()

        def done(self):
            if not self.sent:
                self.send.wait_send()
                self.sent = True

    links = []

    def post(src, dst, target, landing=None):
        link = Link(src, dst, target, landing).start()
        links.append(link)
        return link

    small = [pltpu.make_async_copy(a, b, ssem.at[new_sem()])
             for a, b in ((scale_in, scale), (shift_in, shift), (gain_in, gain))]
    for copy in small:
        copy.start()

    barrier = pltpu.get_barrier_semaphore()
    for k in range(NX):
        for cc in range(2):
            if k == 0 and cc == 0:
                continue
            pl.semaphore_signal(barrier, inc=1, device_id=dev(xat(k), z, y, lax.rem(c + cc, 2)),
                                device_id_type=MESH)
    for k in range(1, NZ):
        pl.semaphore_signal(barrier, inc=1, device_id=to_z(k), device_id_type=MESH)
    for k in range(1, NY):
        pl.semaphore_signal(barrier, inc=1, device_id=to_y(k), device_id_type=MESH)

    @pl.when(z // 4 != xl)
    def _():
        pl.semaphore_signal(barrier, inc=1, device_id=dev(2 * c + xh, zat(4), y, 1), device_id_type=MESH)

    pl.semaphore_wait(barrier, 2 * NX - 1 + NZ - 1 + NY - 1 + c)

    partner = dev(xh * 2 + c, z, y, xl)

    class Swap:
        def __init__(self, src, here, there):
            n = new_sem()
            self.local = pltpu.make_async_copy(src, here, ssem.at[n])
            self.remote = pltpu.make_async_remote_copy(
                src_ref=src, dst_ref=there, send_sem=ssem.at[n], recv_sem=rsem.at[n],
                device_id=partner, device_id_type=MESH)
            self.landing = pltpu.make_async_remote_copy(
                src_ref=here, dst_ref=here, send_sem=ssem.at[n], recv_sem=rsem.at[n],
                device_id=partner, device_id_type=MESH)

        def start(self):
            @pl.when(stays)
            def _():
                self.local.start()

            @pl.when(jnp.logical_not(stays))
            def _():
                self.remote.start()
            return self

        def wait(self):
            @pl.when(stays)
            def _():
                self.local.wait()

            @pl.when(jnp.logical_not(stays))
            def _():
                self.remote.wait_send()
                self.landing.wait_recv()

    in_q = Swap(w_in.at[pl.ds(0, 1)], wbuf.at[pl.ds(0, 1), c, z, y], wbuf.at[pl.ds(0, 1), oc, z, y]).start()
    in_k = Swap(k_in, kv.at[0, c, z], kv.at[0, oc, z]).start()
    in_v = Swap(v_in, kv.at[1, c, z], kv.at[1, oc, z]).start()
    in_kv = Swap(w_in.at[pl.ds(1, 2)], wbuf.at[pl.ds(1, 2), c, z, y], wbuf.at[pl.ds(1, 2), oc, z, y]).start()

    wo_x, wo_c = 2 * xl + z // 4, xh
    wo_self = jnp.logical_and(jnp.logical_and(wo_x == x, wo_c == c), c == 0)
    wo_sem = new_sem()

    def wo_blk(zz, ys):
        group = 2 * c + jnp.where(zz // 4 == xl, 0, 1)
        return wo.at[group, lax.rem(zz, 4), ys]

    def wo_first(landing):
        dst = wo.at[h, lax.rem(z, 4), y]
        if landing:
            dst = wo_blk(z, y)
        return pltpu.make_async_remote_copy(
            src_ref=wo_in, dst_ref=dst, send_sem=ssem.at[wo_sem], recv_sem=rsem.at[wo_sem],
            device_id=dev(wo_x, lax.rem(z + 4 * c, NZ), y, wo_c), device_id_type=MESH)

    wo_local = pltpu.make_async_copy(wo_in, wo.at[h, lax.rem(z, 4), y], ssem.at[wo_sem])

    @pl.when(wo_self)
    def _():
        wo_local.start()

    @pl.when(jnp.logical_not(wo_self))
    def _():
        wo_first(False).start()

    tok_sem = [new_sem(), new_sem()]
    tok_local = pltpu.make_async_copy(tokens, tok, ssem.at[tok_sem[0]])

    def tok_copy(k):
        rows = pl.ds(0, 64) if k == 0 else pl.ds(64, 128)
        xo = x + 1 - 2 * xl if k == 0 else lax.rem(x + 3 + 2 * xl, NX)
        return pltpu.make_async_remote_copy(
            src_ref=tokens.at[rows], dst_ref=tok.at[rows], send_sem=ssem.at[tok_sem[k]],
            recv_sem=rsem.at[tok_sem[k]], device_id=dev(xo, z, y, oc), device_id_type=MESH)

    @pl.when(stays)
    def _():
        tok_local.start()

    @pl.when(jnp.logical_not(stays))
    def _():
        tok_copy(0).start()
        tok_copy(1).start()

    in_g = Swap(gate, gbuf, gbuf).start()

    in_q.wait()
    wq_z = []
    for k in (1, -1, 2, -2, 3, -3, 4):
        wq_z.append(post(wbuf.at[0, c, z, y], wbuf.at[0, c, z, y], to_z(k),
                         landing=wbuf.at[0, c, zat(-k), y]))

    def ring(block, first, second):
        state = {}

        def step(s):
            if s > 0:
                for link in state[s - 1]:
                    link.arrived()
            if s > 3:
                return
            if s < 3:
                right = post(block(zat(-s)), block(zat(-s)), to_z(1), landing=block(zat(-1 - s)))
                left = post(block(zat(s)), block(zat(s)), to_z(-1), landing=block(zat(1 + s)))
            else:
                right = post(first(zat(-s)), first(zat(-s)), to_z(1), landing=first(zat(-1 - s)))
                left = post(second(zat(s)), second(zat(s)), to_z(-1), landing=second(zat(1 + s)))
            state[s] = (right, left)
        return step, state

    wkv_step, _ = ring(lambda b: wbuf.at[pl.ds(1, 2), c, b, y],
                    lambda b: wbuf.at[pl.ds(1, 1), c, b, y],
                    lambda b: wbuf.at[pl.ds(2, 1), c, b, y])
    kv_ring, kv_state = ring(lambda b: kv.at[:, c, b],
                   lambda b: kv.at[pl.ds(0, 1), c, b],
                   lambda b: kv.at[pl.ds(1, 1), c, b])
    kv_sib = []

    def kv_share(b):
        kv_sib.append(post(kv.at[:, c, b], kv.at[:, c, b], sibling, landing=kv.at[:, oc, b]))

    def kv_step(s):
        kv_ring(s)
        if s == 0:
            kv_share(z)
        elif s < 4:
            kv_share(zat(-s))
            kv_share(zat(s))
        else:
            kv_share(zat(4))

    def w_y(i):
        st = {}
        sib = []

        def share(b):
            sib.append(post(wbuf.at[i, c, :, b], wbuf.at[i, c, :, b], sibling,
                            landing=wbuf.at[i, oc, :, b]))

        def begin():
            src = wbuf.at[i, c, :, y]
            st["r"] = post(src, src, to_y(1), landing=wbuf.at[i, c, :, yat(-1)])
            st["l"] = post(src, src, to_y(-1), landing=wbuf.at[i, c, :, yat(1)])
            share(y)

        def middle():
            lo, hi = pl.ds(0, 4), pl.ds(4, 4)
            st["r"].arrived()
            src = wbuf.at[i, c, lo, yat(-1)]
            st["rr"] = post(src, src, to_y(1), landing=wbuf.at[i, c, lo, yat(2)])
            st["l"].arrived()
            src = wbuf.at[i, c, hi, yat(1)]
            st["ll"] = post(src, src, to_y(-1), landing=wbuf.at[i, c, hi, yat(2)])
            share(yat(-1))
            share(yat(1))

        def end():
            st["rr"].arrived()
            st["ll"].arrived()
            share(yat(2))

        def ready():
            for link in sib:
                link.arrived()
        return begin, middle, end, ready

    q_begin, q_middle, q_end, q_ready = w_y(0)
    k_begin, k_middle, k_end, k_ready = w_y(1)
    v_begin, v_middle, v_end, v_ready = w_y(2)

    in_k.wait()
    in_v.wait()
    kv_step(0)
    in_kv.wait()
    wkv_step(0)

    @pl.when(wo_self)
    def _():
        wo_local.wait()

    @pl.when(jnp.logical_not(wo_self))
    def _():
        wo_first(False).wait_send()
        wo_first(True).wait_recv()

    wo_y = [post(wo_blk(z, y), wo_blk(z, y), to_y(d), landing=wo_blk(z, yat(-d))) for d in (1, 3, 2)]
    every = pl.ds(0, NY)
    lo_y, hi_y = pl.ds(0, 2), pl.ds(2, 2)
    wo_step, _ = ring(lambda b: wo_blk(b, every), lambda b: wo_blk(b, lo_y), lambda b: wo_blk(b, hi_y))

    rows_i = lax.broadcasted_iota(jnp.int32, (ROWS, HD), 0)
    lanes_i = lax.broadcasted_iota(jnp.int32, (ROWS, HD), 1)
    for s in range(16):
        limit = counts[s * NY + y]
        keep = jnp.logical_or(rows_i < limit, lanes_i > 0)
        mask[s] = jnp.where(keep, 0.0, NEG).astype(BF16)

    wkv_step(1)
    for link in wq_z:
        link.arrived()
    q_begin()
    wkv_step(2)

    @pl.when(stays)
    def _():
        tok_local.wait()

    @pl.when(jnp.logical_not(stays))
    def _():
        tok_copy(0).wait()
        tok_copy(1).wait()

    for copy in small:
        copy.wait()

    def modulate(i, carry):
        r = pl.ds(pl.multiple_of(i * 16, 16), 16)
        t = tok[r, :].astype(F32)
        mean = jnp.mean(t, axis=1, keepdims=True)
        t = t - mean
        var = jnp.mean(t * t, axis=1, keepdims=True)
        t = t * lax.rsqrt(var + 1e-6)
        xmod[r, :] = (t * (1.0 + scale[...]) + shift[...]).astype(BF16)
        return carry

    lax.fori_loop(0, ROWS // 16, modulate, 0)
    wkv_step(3)
    kv_step(1)
    q_middle()
    wkv_step(4)
    q_end()
    k_begin()
    kv_step(2)
    q_ready()

    def project(i):
        return jnp.dot(xmod[...], wbuf[i].reshape(D, HQ), preferred_element_type=F32)

    def head_norm(r):
        return r / jnp.sqrt(jnp.mean(r * r, axis=1, keepdims=True) + 1e-6)

    raw = project(0)
    for j in range(3):
        cols = slice(j * HD, (j + 1) * HD)
        qbuf[y, :, cols] = (head_norm(raw[:, cols]) * gain[...]).astype(BF16)
    q_links = {}
    for d in (1, 3, 2):
        q_links[d] = post(qbuf.at[y], qbuf.at[y], to_y(d), landing=qbuf.at[yat(-d)])
    ones = jnp.ones((768, HD), BF16)

    lane = lax.broadcasted_iota(jnp.int32, (ROWS, HD), 1)

    def absorb(j, zs, fresh_start):
        cols = pl.ds(pl.multiple_of(j * HD, HD), HD)
        q = jnp.concatenate([qbuf[y, :, cols], jnp.where(lane == 0, 1.0, 0.0).astype(BF16)], axis=1)
        places = [(cc, zz) for cc in range(2) for zz in zs]
        kb = jnp.concatenate(
            [jnp.concatenate([kv[0, cc, zz, :, cols], mask[cc * NZ + zz]], axis=1) for cc, zz in places],
            axis=0)
        s = lax.dot_general(q, kb, (((1,), (1,)), ((), ())), preferred_element_type=F32)
        top = s[:, :HD]
        for t in range(1, 6):
            top = jnp.maximum(top, s[:, t * HD:(t + 1) * HD])
        m = jnp.max(top, axis=1, keepdims=True)
        if not fresh_start:
            old = run_m[j][:, :1]
            m = jnp.maximum(m, old)
        w = jnp.exp2((s - m) * C2).astype(BF16)
        vb = jnp.concatenate([kv[1, cc, zz, :, cols] for cc, zz in places], axis=0)
        acc = jnp.dot(w, jnp.concatenate([vb, ones], axis=1), preferred_element_type=F32)
        if not fresh_start:
            acc = acc + run_acc[j] * jnp.exp2((old - m) * C2)
        run_m[j] = jnp.broadcast_to(m, (ROWS, HD))
        run_acc[j] = acc

    def absorb_all(zs, fresh_start):
        def one(j, carry):
            absorb(j, zs, fresh_start)
            return carry
        lax.fori_loop(0, 3, one, 0)

    others = (1, 3, 2)
    wide = len(others) * ROWS
    lane_w = lax.broadcasted_iota(jnp.int32, (wide, HD), 1)

    def remote_head(j):
        cols = slice(j * HD, (j + 1) * HD)
        q = jnp.concatenate([qbuf[yat(d), :, cols] for d in others], axis=0)
        q = jnp.concatenate([q, jnp.where(lane_w == 0, 1.0, 0.0).astype(BF16)], axis=1)

        def scores(b):
            cc, zz = b // 2, 4 * (b % 2)
            kb = jnp.concatenate([kv[0, cc, zz:zz + 4, :, cols].reshape(768, HD),
                                  mask[4 * b:4 * b + 4].reshape(768, HD)], axis=1)
            return lax.dot_general(q, kb, (((1,), (1,)), ((), ())), preferred_element_type=F32)

        m, acc, s = None, None, scores(0)
        for b in range(4):
            ahead = scores(b + 1) if b < 3 else None
            top = s[:, :HD]
            for t in range(1, 6):
                top = jnp.maximum(top, s[:, t * HD:(t + 1) * HD])
            new = jnp.max(top, axis=1, keepdims=True)
            if m is not None:
                new = jnp.maximum(new, m)
            w = jnp.exp2((s - new) * C2).astype(BF16)
            cc, zz = b // 2, 4 * (b % 2)
            vb = jnp.concatenate([kv[1, cc, zz:zz + 4, :, cols].reshape(768, HD), ones], axis=1)
            pv = jnp.dot(w, vb, preferred_element_type=F32)
            acc = pv if m is None else acc * jnp.exp2((m - new) * C2) + pv
            m, s = new, ahead
        total = acc[:, HD:]
        o = (acc[:, :HD] / total).astype(BF16)
        lse = m * C2 + jnp.log2(total)
        stat[...] = jnp.where(lane_w % 4 == j, lse, 0.0 if j == 0 else stat[...])
        for n, d in enumerate(others):
            osend[d, j] = o[n * ROWS:(n + 1) * ROWS]
            o_links.append(post(osend.at[d, j], orecv.at[d, j], to_y(d)))
        if j == 2:
            full = stat[...]
            top = full.astype(BF16).astype(F32)
            mid = (full - top).astype(BF16).astype(F32)
            low = full - top - mid
            packed = jnp.where(lane_w < 4, top, jnp.where(lane_w < 8, mid, low)).astype(BF16)
            for n, d in enumerate(others):
                osend[d, 3] = packed[n * ROWS:(n + 1) * ROWS]
                o_links.append(post(osend.at[d, 3], orecv.at[d, 3], to_y(d)))

    o_links = []
    kv_sib[1].arrived()
    kv_sib[2].arrived()
    absorb_all((zat(-1), zat(1)), True)
    kv_step(3)
    kv_sib[3].arrived()
    kv_sib[4].arrived()
    absorb_all((zat(-2), zat(2)), False)
    kv_step(4)
    for link in wo_y:
        link.arrived()
    wo_step(0)
    k_middle()
    v_begin()
    kv_sib[5].arrived()
    kv_sib[6].arrived()
    absorb_all((zat(-3), zat(3)), False)
    kv_sib[0].arrived()
    kv_sib[7].arrived()
    for link in q_links.values():
        link.arrived()
    remote_head(0)
    k_end()
    v_middle()
    wo_step(1)
    remote_head(1)
    v_end()
    wo_step(2)
    remote_head(2)
    k_ready()
    raw = project(1)
    for j in range(3):
        cols = slice(j * HD, (j + 1) * HD)
        mix[:, cols] = head_norm(raw[:, cols]).astype(BF16)
    wo_step(3)
    v_ready()
    mix[:, HQ:] = project(2).astype(BF16)

    for link in kv_state[0] + (kv_sib[0],):
        link.done()
    kv[0, c, z] = mix[:, :HQ]
    kv[1, c, z] = mix[:, HQ:]
    wo_step(4)
    blk = wo.at[pl.ds(2 * c, 2)]
    wo_s = post(blk, blk, sibling, landing=wo.at[pl.ds(2 * oc, 2)])

    for j in range(3):
        absorb(j, (z, zat(4)), False)
    for link in o_links:
        link.arrived()
    att_links = []
    for j in range(3):
        cols = slice(j * HD, (j + 1) * HD)
        total = run_acc[j][:, HD:]
        parts = [run_acc[j][:, :HD] / total]
        lses = [run_m[j][:, :1] * C2 + jnp.log2(total[:, :1])]
        for d in (1, 3, 2):
            parts.append(orecv[d, j].astype(F32))
            st = jnp.where(jnp.logical_and(lane % 4 == j, lane < 12), orecv[d, 3].astype(F32), 0.0)
            lses.append(jnp.sum(st, axis=1, keepdims=True))
        top = functools.reduce(jnp.maximum, lses)
        ws = [jnp.exp2(v - top) for v in lses]
        total = functools.reduce(jnp.add, ws)
        mixd = functools.reduce(jnp.add, [w * o for w, o in zip(ws, parts)])
        att[x, :, cols] = (mixd / total).astype(BF16)
        for k in (1, 3, 2):
            att_links.append(post(att.at[x, :, pl.ds(j * HD, HD)], att.at[x, :, pl.ds(j * HD, HD)],
                                  dev(xat(k), z, y, c),
                                  landing=att.at[xat(-k), :, pl.ds(j * HD, HD)]))
    wo_s.arrived()
    in_g.wait()
    for link in att_links:
        link.arrived()
    last = []
    for n in range(3):
        acc = jnp.zeros((ROWS, 256), F32)
        for g in range(NX):
            wt = wo[g].reshape(768, HQ)[n * 256:(n + 1) * 256]
            acc = acc + lax.dot_general(att[g], wt, (((1,), (1,)), ((), ())),
                                        preferred_element_type=F32)
        cols = slice(n * 256, (n + 1) * 256)
        mix[:, cols] = (acc * gbuf[:, cols]).astype(BF16)
        part = pl.ds(n * 256, 256)
        last.append(Swap(mix.at[:, part], out.at[:, part], out.at[:, part]).start())
    for swap in last:
        swap.wait()
    for link in links:
        link.done()
    assert next_sem[0] <= N_SEM, next_sem[0]


def shards(tokens, valid_counts, mod_shift, mod_scale, mod_gate, q_gain, w_qkv, w_out,
           stale_keys, stale_values):
    hbm = pl.BlockSpec(memory_space=pltpu.HBM)
    return pl.pallas_call(
        kernel,
        out_shape=jax.ShapeDtypeStruct((ROWS, 768), BF16),
        in_specs=[pl.BlockSpec(memory_space=pltpu.SMEM)] + [hbm] * 9,
        out_specs=hbm,
        scratch_shapes=[
            pltpu.VMEM((ROWS, D), BF16),
            pltpu.VMEM((1, D), F32),
            pltpu.VMEM((1, D), F32),
            pltpu.VMEM((1, HD), F32),
            pltpu.VMEM((ROWS, D), BF16),
            pltpu.VMEM((3, 2, NZ, NY, SHARD, HQ), BF16),
            pltpu.VMEM((2, 2, NZ, ROWS, HQ), BF16),
            pltpu.VMEM((16, ROWS, HD), BF16),
            pltpu.VMEM((NY, ROWS, HQ), BF16),
            pltpu.VMEM((3 * ROWS, HD), F32),
            pltpu.VMEM((NY, 4, ROWS, HD), BF16),
            pltpu.VMEM((NY, 4, ROWS, HD), BF16),
            pltpu.VMEM((NX, ROWS, HQ), BF16),
            pltpu.VMEM((4, 4, NY, SHARD, HQ), BF16),
            pltpu.VMEM((1, 768), F32),
            pltpu.VMEM((ROWS, 768), BF16),
            pltpu.VMEM((3, ROWS, HD), F32),
            pltpu.VMEM((3, ROWS, 2 * HD), F32),
            pltpu.SemaphoreType.DMA((N_SEM,)),
            pltpu.SemaphoreType.DMA((N_SEM,)),
        ],
        compiler_params=pltpu.CompilerParams(
            collective_id=0, has_side_effects=True, vmem_limit_bytes=63 * 2**20),
    )(valid_counts, tokens, mod_scale.reshape(1, D), mod_shift.reshape(1, D),
      q_gain.reshape(1, HD), mod_gate.reshape(1, 768), jnp.transpose(w_qkv, (1, 0, 2)),
      jnp.transpose(w_out), stale_keys, stale_values)


def solution(mesh):
    in_specs = (
        P("patch", None), P(), P(), P(), P("head"), P(), P("patch", None, "head"),
        P("head", "patch"), P("patch", "head"), P("patch", "head"),
    )
    return jax.shard_map(shards, mesh=mesh, in_specs=in_specs, out_specs=P("patch", "head"),
                         check_vma=False)
```

```python
import functools
import math

import jax
import jax.numpy as jnp
from jax import lax
from jax.experimental import pallas as pl
from jax.experimental.pallas import tpu as pltpu
from jax.sharding import PartitionSpec as P

MESH = pl.DeviceIdType.MESH
F32 = jnp.float32
BF16 = jnp.bfloat16
ROWS = 192
D = 3072
HQ = 384
HD = 128
NZ, NY, NX = 8, 4, 4
SHARD = 48
C2 = math.log2(math.e) / math.sqrt(HD)
NEG = -1e30
N_SEM = 168


def dev(x, z, y, c):
    return ((lax.rem(x, 2) * NZ + z) * NY + y, (x // 2) * 2 + c)


def kernel(counts, tokens, scale_in, shift_in, gain_in, gate, w_in, wo_in, k_in, v_in, out,
           tok, scale, shift, gain, xmod, wbuf, kv, mask, qbuf, stat, osend, orecv, att, wo, gbuf, mix,
           run_m, run_acc, ssem, rsem):
    p = lax.axis_index("patch")
    h = lax.axis_index("head")
    xl, z, y = p // (NZ * NY), lax.rem(p // NY, NZ), lax.rem(p, NY)
    xh, c = h // 2, lax.rem(h, 2)
    x = xh * 2 + xl
    oc = 1 - c

    def zat(k):
        return lax.rem(z + k + NZ, NZ)

    def yat(k):
        return lax.rem(y + k + NY, NY)

    def xat(k):
        return lax.rem(x + k + NX, NX)

    def to_z(k):
        return dev(x, zat(k), y, c)

    def to_y(k):
        return dev(x, z, yat(k), c)

    sibling = dev(x, z, y, oc)
    stays = c == xl

    next_sem = [0]

    def new_sem():
        next_sem[0] += 1
        return next_sem[0] - 1

    class Link:
        def __init__(self, src, dst, target, landing=None):
            n = new_sem()
            self.send = pltpu.make_async_remote_copy(
                src_ref=src, dst_ref=dst, send_sem=ssem.at[n], recv_sem=rsem.at[n],
                device_id=target, device_id_type=MESH)
            land = dst if landing is None else landing
            self.recv = pltpu.make_async_remote_copy(
                src_ref=land, dst_ref=land, send_sem=ssem.at[n], recv_sem=rsem.at[n],
                device_id=target, device_id_type=MESH)
            self.n = n
            self.sent = False

        def start(self):
            self.send.start()
            return self

        def arrived(self):
            self.recv.wait_recv()

        def done(self):
            if not self.sent:
                self.send.wait_send()
                self.sent = True

    links = []

    def post(src, dst, target, landing=None):
        link = Link(src, dst, target, landing).start()
        links.append(link)
        return link

    small = [pltpu.make_async_copy(a, b, ssem.at[new_sem()])
             for a, b in ((scale_in, scale), (shift_in, shift), (gain_in, gain))]
    for copy in small:
        copy.start()

    barrier = pltpu.get_barrier_semaphore()
    for k in range(NX):
        for cc in range(2):
            if k == 0 and cc == 0:
                continue
            pl.semaphore_signal(barrier, inc=1, device_id=dev(xat(k), z, y, lax.rem(c + cc, 2)),
                                device_id_type=MESH)
    for k in range(1, NZ):
        pl.semaphore_signal(barrier, inc=1, device_id=to_z(k), device_id_type=MESH)
    for k in range(1, NY):
        pl.semaphore_signal(barrier, inc=1, device_id=to_y(k), device_id_type=MESH)

    @pl.when(z // 4 != xl)
    def _():
        pl.semaphore_signal(barrier, inc=1, device_id=dev(2 * c + xh, zat(4), y, 1), device_id_type=MESH)

    pl.semaphore_wait(barrier, 2 * NX - 1 + NZ - 1 + NY - 1 + c)

    partner = dev(xh * 2 + c, z, y, xl)

    class Swap:
        def __init__(self, src, here, there):
            n = new_sem()
            self.local = pltpu.make_async_copy(src, here, ssem.at[n])
            self.remote = pltpu.make_async_remote_copy(
                src_ref=src, dst_ref=there, send_sem=ssem.at[n], recv_sem=rsem.at[n],
                device_id=partner, device_id_type=MESH)
            self.landing = pltpu.make_async_remote_copy(
                src_ref=here, dst_ref=here, send_sem=ssem.at[n], recv_sem=rsem.at[n],
                device_id=partner, device_id_type=MESH)

        def start(self):
            @pl.when(stays)
            def _():
                self.local.start()

            @pl.when(jnp.logical_not(stays))
            def _():
                self.remote.start()
            return self

        def wait(self):
            @pl.when(stays)
            def _():
                self.local.wait()

            @pl.when(jnp.logical_not(stays))
            def _():
                self.remote.wait_send()
                self.landing.wait_recv()

    in_q = Swap(w_in.at[pl.ds(0, 1)], wbuf.at[pl.ds(0, 1), c, z, y], wbuf.at[pl.ds(0, 1), oc, z, y]).start()
    in_k = Swap(k_in, kv.at[0, c, z], kv.at[0, oc, z]).start()
    in_v = Swap(v_in, kv.at[1, c, z], kv.at[1, oc, z]).start()
    in_kv = Swap(w_in.at[pl.ds(1, 2)], wbuf.at[pl.ds(1, 2), c, z, y], wbuf.at[pl.ds(1, 2), oc, z, y]).start()

    wo_x, wo_c = 2 * xl + z // 4, xh
    wo_self = jnp.logical_and(jnp.logical_and(wo_x == x, wo_c == c), c == 0)
    wo_sem = new_sem()

    def wo_blk(zz, ys, cc=c):
        group = 2 * cc + jnp.where(zz // 4 == xl, 0, 1)
        return wo.at[group, lax.rem(zz, 4), ys]

    def wo_first(landing):
        dst = wo.at[h, lax.rem(z, 4), y]
        if landing:
            dst = wo_blk(z, y)
        return pltpu.make_async_remote_copy(
            src_ref=wo_in, dst_ref=dst, send_sem=ssem.at[wo_sem], recv_sem=rsem.at[wo_sem],
            device_id=dev(wo_x, lax.rem(z + 4 * c, NZ), y, wo_c), device_id_type=MESH)

    wo_local = pltpu.make_async_copy(wo_in, wo.at[h, lax.rem(z, 4), y], ssem.at[wo_sem])

    @pl.when(wo_self)
    def _():
        wo_local.start()

    @pl.when(jnp.logical_not(wo_self))
    def _():
        wo_first(False).start()

    tok_sem = [new_sem(), new_sem()]
    tok_local = pltpu.make_async_copy(tokens, tok, ssem.at[tok_sem[0]])

    def tok_copy(k):
        rows = pl.ds(0, 64) if k == 0 else pl.ds(64, 128)
        xo = x + 1 - 2 * xl if k == 0 else lax.rem(x + 3 + 2 * xl, NX)
        return pltpu.make_async_remote_copy(
            src_ref=tokens.at[rows], dst_ref=tok.at[rows], send_sem=ssem.at[tok_sem[k]],
            recv_sem=rsem.at[tok_sem[k]], device_id=dev(xo, z, y, oc), device_id_type=MESH)

    @pl.when(stays)
    def _():
        tok_local.start()

    @pl.when(jnp.logical_not(stays))
    def _():
        tok_copy(0).start()
        tok_copy(1).start()

    in_g = Swap(gate, gbuf, gbuf).start()

    in_q.wait()
    wq_z = []
    for k in (1, -1, 2, -2, 3, -3, 4):
        wq_z.append(post(wbuf.at[0, c, z, y], wbuf.at[0, c, z, y], to_z(k),
                         landing=wbuf.at[0, c, zat(-k), y]))

    def ring(block, first, second):
        state = {}

        def step(s):
            if s > 0:
                for link in state[s - 1]:
                    link.arrived()
            if s > 3:
                return
            if s < 3:
                right = post(block(zat(-s)), block(zat(-s)), to_z(1), landing=block(zat(-1 - s)))
                left = post(block(zat(s)), block(zat(s)), to_z(-1), landing=block(zat(1 + s)))
            else:
                right = post(first(zat(-s)), first(zat(-s)), to_z(1), landing=first(zat(-1 - s)))
                left = post(second(zat(s)), second(zat(s)), to_z(-1), landing=second(zat(1 + s)))
            state[s] = (right, left)
        return step, state

    def shared_ring(block, first, second):
        hop, state = ring(lambda b: block(b, c), first, second)
        shares = []

        def share(b):
            shares.append(post(block(b, c), block(b, c), sibling, landing=block(b, oc)))

        def step(s):
            hop(s)
            if s == 0:
                share(z)
            elif s < 4:
                share(zat(-s))
                share(zat(s))
            else:
                share(zat(4))
        return step, state, shares

    wk_step, _ = ring(lambda b: wbuf.at[1, c, b, y], lambda b: wbuf.at[1, c, b, y, pl.ds(0, 16)],
                      lambda b: wbuf.at[1, c, b, y, pl.ds(16, 32)])
    upper, lower = pl.ds(0, ROWS // 2), pl.ds(ROWS // 2, ROWS // 2)
    key_step, key_state, key_sib = shared_ring(
        lambda b, cc: kv.at[0, cc, b], lambda b: kv.at[0, c, b, upper], lambda b: kv.at[0, c, b, lower])
    val_step, val_state, val_sib = shared_ring(
        lambda b, cc: kv.at[1, cc, b], lambda b: kv.at[1, c, b, upper], lambda b: kv.at[1, c, b, lower])

    def kv_step(s):
        key_step(s)
        val_step(s)

    def kv_wait(*which):
        for i in which:
            key_sib[i].arrived()
            val_sib[i].arrived()

    lo_y, hi_y = pl.ds(0, 2), pl.ds(2, 2)
    wv_step, _, wv_sib = shared_ring(
        lambda b, cc: wbuf.at[2, cc, b], lambda b: wbuf.at[2, c, b, lo_y], lambda b: wbuf.at[2, c, b, hi_y])
    wo_step, _ = ring(lambda b: wo_blk(b, y), lambda b: wo_blk(b, y).at[pl.ds(0, 16)],
                      lambda b: wo_blk(b, y).at[pl.ds(16, 32)])

    def round_y(block, low, high):
        st = {}
        sib = []

        def share(b):
            sib.append(post(block(c, b), block(c, b), sibling, landing=block(oc, b)))

        def begin():
            src = block(c, y)
            st["r"] = post(src, src, to_y(1), landing=block(c, yat(-1)))
            st["l"] = post(src, src, to_y(-1), landing=block(c, yat(1)))
            share(y)

        def middle():
            st["r"].arrived()
            st["rr"] = post(low(yat(-1)), low(yat(-1)), to_y(1), landing=low(yat(2)))
            st["l"].arrived()
            st["ll"] = post(high(yat(1)), high(yat(1)), to_y(-1), landing=high(yat(2)))
            share(yat(-1))
            share(yat(1))

        def end():
            st["rr"].arrived()
            st["ll"].arrived()
            share(yat(2))

        def ready():
            for link in sib:
                link.arrived()
        return begin, middle, end, ready

    def w_y(i):
        return round_y(lambda cc, b: wbuf.at[i, cc, :, b], lambda b: wbuf.at[i, c, pl.ds(0, 4), b],
                       lambda b: wbuf.at[i, c, pl.ds(4, 4), b])

    wo_rows = pl.ds(2 * c, 2)
    wo_begin, wo_middle, wo_end, wo_ready = round_y(
        lambda cc, b: wo.at[pl.ds(2 * cc, 2), :, b], lambda b: wo.at[wo_rows, pl.ds(0, 2), b],
        lambda b: wo.at[wo_rows, pl.ds(2, 2), b])
    q_begin, q_middle, q_end, q_ready = w_y(0)
    k_begin, k_middle, k_end, k_ready = w_y(1)

    in_kv.wait()
    wk_step(0)
    wv_y = [post(wbuf.at[2, c, z, y], wbuf.at[2, c, z, y], to_y(d), landing=wbuf.at[2, c, z, yat(-d)])
            for d in (1, 3, 2)]

    @pl.when(wo_self)
    def _():
        wo_local.wait()

    @pl.when(jnp.logical_not(wo_self))
    def _():
        wo_first(False).wait_send()
        wo_first(True).wait_recv()

    wo_step(0)

    rows_i = lax.broadcasted_iota(jnp.int32, (ROWS, HD), 0)
    lanes_i = lax.broadcasted_iota(jnp.int32, (ROWS, HD), 1)
    for s in range(16):
        limit = counts[s * NY + y]
        keep = jnp.logical_or(rows_i < limit, lanes_i > 0)
        mask[s] = jnp.where(keep, 0.0, NEG).astype(BF16)

    wk_step(1)
    wo_step(1)
    in_k.wait()
    in_v.wait()
    for link in wq_z:
        link.arrived()
    q_begin()
    kv_step(0)
    wk_step(2)
    wo_step(2)

    @pl.when(stays)
    def _():
        tok_local.wait()

    @pl.when(jnp.logical_not(stays))
    def _():
        tok_copy(0).wait()
        tok_copy(1).wait()

    for copy in small:
        copy.wait()

    def modulate(i, carry):
        r = pl.ds(pl.multiple_of(i * 16, 16), 16)
        t = tok[r, :].astype(F32)
        mean = jnp.mean(t, axis=1, keepdims=True)
        t = t - mean
        var = jnp.mean(t * t, axis=1, keepdims=True)
        t = t * lax.rsqrt(var + 1e-6)
        xmod[r, :] = (t * (1.0 + scale[...]) + shift[...]).astype(BF16)
        return carry

    lax.fori_loop(0, ROWS // 16, modulate, 0)
    wk_step(3)
    wo_step(3)
    q_middle()
    wk_step(4)
    kv_step(1)
    q_end()
    k_begin()
    q_ready()
    kv_step(2)

    def project(i):
        return jnp.dot(xmod[...], wbuf[i].reshape(D, HQ), preferred_element_type=F32)

    def head_norm(r):
        return r / jnp.sqrt(jnp.mean(r * r, axis=1, keepdims=True) + 1e-6)

    raw = project(0)
    for j in range(3):
        cols = slice(j * HD, (j + 1) * HD)
        qbuf[y, :, cols] = (head_norm(raw[:, cols]) * gain[...]).astype(BF16)
    q_links = {}
    for d in (1, 3, 2):
        q_links[d] = post(qbuf.at[y], qbuf.at[y], to_y(d), landing=qbuf.at[yat(-d)])
    ones = jnp.ones((768, HD), BF16)

    lane = lax.broadcasted_iota(jnp.int32, (ROWS, HD), 1)

    def absorb(j, zs, fresh_start):
        cols = pl.ds(pl.multiple_of(j * HD, HD), HD)
        q = jnp.concatenate([qbuf[y, :, cols], jnp.where(lane == 0, 1.0, 0.0).astype(BF16)], axis=1)
        places = [(cc, zz) for cc in range(2) for zz in zs]
        kb = jnp.concatenate(
            [jnp.concatenate([kv[0, cc, zz, :, cols], mask[cc * NZ + zz]], axis=1) for cc, zz in places],
            axis=0)
        s = lax.dot_general(q, kb, (((1,), (1,)), ((), ())), preferred_element_type=F32)
        top = s[:, :HD]
        for t in range(1, 6):
            top = jnp.maximum(top, s[:, t * HD:(t + 1) * HD])
        m = jnp.max(top, axis=1, keepdims=True)
        if not fresh_start:
            old = run_m[j][:, :1]
            m = jnp.maximum(m, old)
        w = jnp.exp2((s - m) * C2).astype(BF16)
        vb = jnp.concatenate([kv[1, cc, zz, :, cols] for cc, zz in places], axis=0)
        acc = jnp.dot(w, jnp.concatenate([vb, ones], axis=1), preferred_element_type=F32)
        if not fresh_start:
            acc = acc + run_acc[j] * jnp.exp2((old - m) * C2)
        run_m[j] = jnp.broadcast_to(m, (ROWS, HD))
        run_acc[j] = acc

    def absorb_all(zs, fresh_start):
        def one(j, carry):
            absorb(j, zs, fresh_start)
            return carry
        lax.fori_loop(0, 3, one, 0)

    others = (1, 3, 2)
    wide = len(others) * ROWS
    lane_w = lax.broadcasted_iota(jnp.int32, (wide, HD), 1)

    def remote_head(j):
        cols = slice(j * HD, (j + 1) * HD)
        q = jnp.concatenate([qbuf[yat(d), :, cols] for d in others], axis=0)
        q = jnp.concatenate([q, jnp.where(lane_w == 0, 1.0, 0.0).astype(BF16)], axis=1)

        def scores(b):
            cc, zz = b // 2, 4 * (b % 2)
            kb = jnp.concatenate([kv[0, cc, zz:zz + 4, :, cols].reshape(768, HD),
                                  mask[4 * b:4 * b + 4].reshape(768, HD)], axis=1)
            return lax.dot_general(q, kb, (((1,), (1,)), ((), ())), preferred_element_type=F32)

        m, acc, s = None, None, scores(0)
        for b in range(4):
            ahead = scores(b + 1) if b < 3 else None
            top = s[:, :HD]
            for t in range(1, 6):
                top = jnp.maximum(top, s[:, t * HD:(t + 1) * HD])
            new = jnp.max(top, axis=1, keepdims=True)
            if m is not None:
                new = jnp.maximum(new, m)
            w = jnp.exp2((s - new) * C2).astype(BF16)
            cc, zz = b // 2, 4 * (b % 2)
            vb = jnp.concatenate([kv[1, cc, zz:zz + 4, :, cols].reshape(768, HD), ones], axis=1)
            pv = jnp.dot(w, vb, preferred_element_type=F32)
            acc = pv if m is None else acc * jnp.exp2((m - new) * C2) + pv
            m, s = new, ahead
        total = acc[:, HD:]
        o = (acc[:, :HD] / total).astype(BF16)
        lse = m * C2 + jnp.log2(total)
        stat[...] = jnp.where(lane_w % 4 == j, lse, 0.0 if j == 0 else stat[...])
        for n, d in enumerate(others):
            osend[d, j] = o[n * ROWS:(n + 1) * ROWS]
            o_links.append(post(osend.at[d, j], orecv.at[d, j], to_y(d)))
        if j == 2:
            full = stat[...]
            top = full.astype(BF16).astype(F32)
            mid = (full - top).astype(BF16).astype(F32)
            low = full - top - mid
            packed = jnp.where(lane_w < 4, top, jnp.where(lane_w < 8, mid, low)).astype(BF16)
            for n, d in enumerate(others):
                osend[d, 3] = packed[n * ROWS:(n + 1) * ROWS]
                o_links.append(post(osend.at[d, 3], orecv.at[d, 3], to_y(d)))

    o_links = []
    kv_wait(1, 2)
    absorb_all((zat(-1), zat(1)), True)
    kv_wait(3, 4)
    absorb_all((zat(-2), zat(2)), False)
    kv_step(3)
    for link in wv_y:
        link.arrived()
    wv_step(0)
    k_middle()
    wo_step(4)
    wo_begin()
    kv_wait(5, 6)
    absorb_all((zat(-3), zat(3)), False)
    kv_step(4)
    wv_step(1)
    kv_wait(0, 7)
    for link in q_links.values():
        link.arrived()
    remote_head(0)
    k_end()
    wv_step(2)
    wo_middle()
    remote_head(1)
    wv_step(3)
    wo_end()
    remote_head(2)
    wv_step(4)
    k_ready()
    raw = project(1)
    for j in range(3):
        cols = slice(j * HD, (j + 1) * HD)
        mix[:, cols] = head_norm(raw[:, cols]).astype(BF16)
    for link in wv_sib:
        link.arrived()
    mix[:, HQ:] = project(2).astype(BF16)

    for link in key_state[0] + val_state[0] + (key_sib[0], val_sib[0]):
        link.done()
    kv[0, c, z] = mix[:, :HQ]
    kv[1, c, z] = mix[:, HQ:]

    for j in range(3):
        absorb(j, (z, zat(4)), False)
    for link in o_links:
        link.arrived()
    att_links = []
    for j in range(3):
        cols = slice(j * HD, (j + 1) * HD)
        total = run_acc[j][:, HD:]
        parts = [run_acc[j][:, :HD] / total]
        lses = [run_m[j][:, :1] * C2 + jnp.log2(total[:, :1])]
        for d in (1, 3, 2):
            parts.append(orecv[d, j].astype(F32))
            st = jnp.where(jnp.logical_and(lane % 4 == j, lane < 12), orecv[d, 3].astype(F32), 0.0)
            lses.append(jnp.sum(st, axis=1, keepdims=True))
        top = functools.reduce(jnp.maximum, lses)
        ws = [jnp.exp2(v - top) for v in lses]
        total = functools.reduce(jnp.add, ws)
        mixd = functools.reduce(jnp.add, [w * o for w, o in zip(ws, parts)])
        att[x, :, cols] = (mixd / total).astype(BF16)
        for k in (1, 3, 2):
            att_links.append(post(att.at[x, :, pl.ds(j * HD, HD)], att.at[x, :, pl.ds(j * HD, HD)],
                                  dev(xat(k), z, y, c),
                                  landing=att.at[xat(-k), :, pl.ds(j * HD, HD)]))
    wo_ready()
    in_g.wait()
    for link in att_links:
        link.arrived()
    last = []
    for n in range(3):
        acc = jnp.zeros((ROWS, 256), F32)
        for g in range(NX):
            wt = wo[g].reshape(768, HQ)[n * 256:(n + 1) * 256]
            acc = acc + lax.dot_general(att[g], wt, (((1,), (1,)), ((), ())),
                                        preferred_element_type=F32)
        cols = slice(n * 256, (n + 1) * 256)
        mix[:, cols] = (acc * gbuf[:, cols]).astype(BF16)
        part = pl.ds(n * 256, 256)
        last.append(Swap(mix.at[:, part], out.at[:, part], out.at[:, part]).start())
    for swap in last:
        swap.wait()
    for link in links:
        link.done()
    assert next_sem[0] <= N_SEM, next_sem[0]


def shards(tokens, valid_counts, mod_shift, mod_scale, mod_gate, q_gain, w_qkv, w_out,
           stale_keys, stale_values):
    hbm = pl.BlockSpec(memory_space=pltpu.HBM)
    return pl.pallas_call(
        kernel,
        out_shape=jax.ShapeDtypeStruct((ROWS, 768), BF16),
        in_specs=[pl.BlockSpec(memory_space=pltpu.SMEM)] + [hbm] * 9,
        out_specs=hbm,
        scratch_shapes=[
            pltpu.VMEM((ROWS, D), BF16),
            pltpu.VMEM((1, D), F32),
            pltpu.VMEM((1, D), F32),
            pltpu.VMEM((1, HD), F32),
            pltpu.VMEM((ROWS, D), BF16),
            pltpu.VMEM((3, 2, NZ, NY, SHARD, HQ), BF16),
            pltpu.VMEM((2, 2, NZ, ROWS, HQ), BF16),
            pltpu.VMEM((16, ROWS, HD), BF16),
            pltpu.VMEM((NY, ROWS, HQ), BF16),
            pltpu.VMEM((3 * ROWS, HD), F32),
            pltpu.VMEM((NY, 4, ROWS, HD), BF16),
            pltpu.VMEM((NY, 4, ROWS, HD), BF16),
            pltpu.VMEM((NX, ROWS, HQ), BF16),
            pltpu.VMEM((4, 4, NY, SHARD, HQ), BF16),
            pltpu.VMEM((1, 768), F32),
            pltpu.VMEM((ROWS, 768), BF16),
            pltpu.VMEM((3, ROWS, HD), F32),
            pltpu.VMEM((3, ROWS, 2 * HD), F32),
            pltpu.SemaphoreType.DMA((N_SEM,)),
            pltpu.SemaphoreType.DMA((N_SEM,)),
        ],
        compiler_params=pltpu.CompilerParams(
            collective_id=0, has_side_effects=True, vmem_limit_bytes=63 * 2**20),
    )(valid_counts, tokens, mod_scale.reshape(1, D), mod_shift.reshape(1, D),
      q_gain.reshape(1, HD), mod_gate.reshape(1, 768), jnp.transpose(w_qkv, (1, 0, 2)),
      jnp.transpose(w_out), stale_keys, stale_values)


def solution(mesh):
    in_specs = (
        P("patch", None), P(), P(), P(), P("head"), P(), P("patch", None, "head"),
        P("head", "patch"), P("patch", "head"), P("patch", "head"),
    )
    return jax.shard_map(shards, mesh=mesh, in_specs=in_specs, out_specs=P("patch", "head"),
                         check_vma=False)
```

```python
import functools
import math

import jax
import jax.numpy as jnp
from jax import lax
from jax.experimental import pallas as pl
from jax.experimental.pallas import tpu as pltpu
from jax.sharding import PartitionSpec as P

MESH = pl.DeviceIdType.MESH
F32 = jnp.float32
BF16 = jnp.bfloat16
ROWS = 192
D = 3072
HQ = 384
HD = 128
NZ, NY, NX = 8, 4, 4
SHARD = 48
C2 = math.log2(math.e) / math.sqrt(HD)
NEG = -1e30
N_SEM = 168


def dev(x, z, y, c):
    return ((lax.rem(x, 2) * NZ + z) * NY + y, (x // 2) * 2 + c)


def kernel(counts, tokens, scale_in, shift_in, gain_in, gate, w_in, wo_in, k_in, v_in, out,
           tok, scale, shift, gain, xmod, wbuf, kv, mask, qbuf, stat, osend, orecv, att, wo, gbuf, mix,
           run_m, run_acc, ssem, rsem):
    p = lax.axis_index("patch")
    h = lax.axis_index("head")
    xl, z, y = p // (NZ * NY), lax.rem(p // NY, NZ), lax.rem(p, NY)
    xh, c = h // 2, lax.rem(h, 2)
    x = xh * 2 + xl
    oc = 1 - c

    def zat(k):
        return lax.rem(z + k + NZ, NZ)

    def yat(k):
        return lax.rem(y + k + NY, NY)

    def xat(k):
        return lax.rem(x + k + NX, NX)

    def to_z(k):
        return dev(x, zat(k), y, c)

    def to_y(k):
        return dev(x, z, yat(k), c)

    sibling = dev(x, z, y, oc)
    stays = c == xl

    next_sem = [0]

    def new_sem():
        next_sem[0] += 1
        return next_sem[0] - 1

    class Link:
        def __init__(self, src, dst, target, landing=None):
            n = new_sem()
            self.send = pltpu.make_async_remote_copy(
                src_ref=src, dst_ref=dst, send_sem=ssem.at[n], recv_sem=rsem.at[n],
                device_id=target, device_id_type=MESH)
            land = dst if landing is None else landing
            self.recv = pltpu.make_async_remote_copy(
                src_ref=land, dst_ref=land, send_sem=ssem.at[n], recv_sem=rsem.at[n],
                device_id=target, device_id_type=MESH)
            self.n = n
            self.sent = False

        def start(self):
            self.send.start()
            return self

        def arrived(self):
            self.recv.wait_recv()

        def done(self):
            if not self.sent:
                self.send.wait_send()
                self.sent = True

    links = []

    def post(src, dst, target, landing=None):
        link = Link(src, dst, target, landing).start()
        links.append(link)
        return link

    small = [pltpu.make_async_copy(a, b, ssem.at[new_sem()])
             for a, b in ((scale_in, scale), (shift_in, shift), (gain_in, gain))]
    for copy in small:
        copy.start()

    barrier = pltpu.get_barrier_semaphore()
    for k in range(NX):
        for cc in range(2):
            if k == 0 and cc == 0:
                continue
            pl.semaphore_signal(barrier, inc=1, device_id=dev(xat(k), z, y, lax.rem(c + cc, 2)),
                                device_id_type=MESH)
    for k in range(1, NZ):
        pl.semaphore_signal(barrier, inc=1, device_id=to_z(k), device_id_type=MESH)
    for k in range(1, NY):
        pl.semaphore_signal(barrier, inc=1, device_id=to_y(k), device_id_type=MESH)

    @pl.when(z // 4 != xl)
    def _():
        pl.semaphore_signal(barrier, inc=1, device_id=dev(2 * c + xh, zat(4), y, 1), device_id_type=MESH)

    pl.semaphore_wait(barrier, 2 * NX - 1 + NZ - 1 + NY - 1 + c)

    partner = dev(xh * 2 + c, z, y, xl)

    class Swap:
        def __init__(self, src, here, there):
            n = new_sem()
            self.local = pltpu.make_async_copy(src, here, ssem.at[n])
            self.remote = pltpu.make_async_remote_copy(
                src_ref=src, dst_ref=there, send_sem=ssem.at[n], recv_sem=rsem.at[n],
                device_id=partner, device_id_type=MESH)
            self.landing = pltpu.make_async_remote_copy(
                src_ref=here, dst_ref=here, send_sem=ssem.at[n], recv_sem=rsem.at[n],
                device_id=partner, device_id_type=MESH)

        def start(self):
            @pl.when(stays)
            def _():
                self.local.start()

            @pl.when(jnp.logical_not(stays))
            def _():
                self.remote.start()
            return self

        def wait(self):
            @pl.when(stays)
            def _():
                self.local.wait()

            @pl.when(jnp.logical_not(stays))
            def _():
                self.remote.wait_send()
                self.landing.wait_recv()

    in_q = Swap(w_in.at[pl.ds(0, 1)], wbuf.at[pl.ds(0, 1), c, z, y], wbuf.at[pl.ds(0, 1), oc, z, y]).start()
    in_k = Swap(k_in, kv.at[0, c, z], kv.at[0, oc, z]).start()
    in_v = Swap(v_in, kv.at[1, c, z], kv.at[1, oc, z]).start()
    in_kv = Swap(w_in.at[pl.ds(1, 2)], wbuf.at[pl.ds(1, 2), c, z, y], wbuf.at[pl.ds(1, 2), oc, z, y]).start()

    wo_x, wo_c = 2 * xl + z // 4, xh
    wo_self = jnp.logical_and(jnp.logical_and(wo_x == x, wo_c == c), c == 0)
    wo_sem = new_sem()

    def wo_blk(zz, ys, cc=c):
        group = 2 * cc + jnp.where(zz // 4 == xl, 0, 1)
        return wo.at[group, lax.rem(zz, 4), ys]

    def wo_first(landing):
        dst = wo.at[h, lax.rem(z, 4), y]
        if landing:
            dst = wo_blk(z, y)
        return pltpu.make_async_remote_copy(
            src_ref=wo_in, dst_ref=dst, send_sem=ssem.at[wo_sem], recv_sem=rsem.at[wo_sem],
            device_id=dev(wo_x, lax.rem(z + 4 * c, NZ), y, wo_c), device_id_type=MESH)

    wo_local = pltpu.make_async_copy(wo_in, wo.at[h, lax.rem(z, 4), y], ssem.at[wo_sem])

    @pl.when(wo_self)
    def _():
        wo_local.start()

    @pl.when(jnp.logical_not(wo_self))
    def _():
        wo_first(False).start()

    tok_sem = [new_sem(), new_sem()]
    tok_local = pltpu.make_async_copy(tokens, tok, ssem.at[tok_sem[0]])

    def tok_copy(k):
        rows = pl.ds(0, 64) if k == 0 else pl.ds(64, 128)
        xo = x + 1 - 2 * xl if k == 0 else lax.rem(x + 3 + 2 * xl, NX)
        return pltpu.make_async_remote_copy(
            src_ref=tokens.at[rows], dst_ref=tok.at[rows], send_sem=ssem.at[tok_sem[k]],
            recv_sem=rsem.at[tok_sem[k]], device_id=dev(xo, z, y, oc), device_id_type=MESH)

    @pl.when(stays)
    def _():
        tok_local.start()

    @pl.when(jnp.logical_not(stays))
    def _():
        tok_copy(0).start()
        tok_copy(1).start()

    in_g = Swap(gate, gbuf, gbuf).start()

    in_q.wait()
    wq_z = []
    for k in (1, -1, 2, -2, 3, -3, 4):
        wq_z.append(post(wbuf.at[0, c, z, y], wbuf.at[0, c, z, y], to_z(k),
                         landing=wbuf.at[0, c, zat(-k), y]))

    def ring(block, first, second):
        state = {}

        def step(s):
            if s > 0:
                for link in state[s - 1]:
                    link.arrived()
            if s > 3:
                return
            if s < 3:
                right = post(block(zat(-s)), block(zat(-s)), to_z(1), landing=block(zat(-1 - s)))
                left = post(block(zat(s)), block(zat(s)), to_z(-1), landing=block(zat(1 + s)))
            else:
                right = post(first(zat(-s)), first(zat(-s)), to_z(1), landing=first(zat(-1 - s)))
                left = post(second(zat(s)), second(zat(s)), to_z(-1), landing=second(zat(1 + s)))
            state[s] = (right, left)
        return step, state

    def shared_ring(block, first, second):
        hop, state = ring(lambda b: block(b, c), first, second)
        shares = []

        def share(b):
            shares.append(post(block(b, c), block(b, c), sibling, landing=block(b, oc)))

        def step(s):
            hop(s)
            if s == 0:
                share(z)
            elif s < 4:
                share(zat(-s))
                share(zat(s))
            else:
                share(zat(4))
        return step, state, shares

    wk_step, _ = ring(lambda b: wbuf.at[1, c, b, y], lambda b: wbuf.at[1, c, b, y, pl.ds(0, 16)],
                      lambda b: wbuf.at[1, c, b, y, pl.ds(16, 32)])
    upper, lower = pl.ds(0, ROWS // 2), pl.ds(ROWS // 2, ROWS // 2)
    key_step, key_state, key_sib = shared_ring(
        lambda b, cc: kv.at[0, cc, b], lambda b: kv.at[0, c, b, upper], lambda b: kv.at[0, c, b, lower])
    val_step, val_state, val_sib = shared_ring(
        lambda b, cc: kv.at[1, cc, b], lambda b: kv.at[1, c, b, upper], lambda b: kv.at[1, c, b, lower])

    def kv_step(s):
        key_step(s)
        val_step(s)

    def kv_wait(*which):
        for i in which:
            key_sib[i].arrived()
            val_sib[i].arrived()

    lo_y, hi_y = pl.ds(0, 2), pl.ds(2, 2)
    wv_step, _, wv_sib = shared_ring(
        lambda b, cc: wbuf.at[2, cc, b], lambda b: wbuf.at[2, c, b, lo_y], lambda b: wbuf.at[2, c, b, hi_y])
    wo_step, _ = ring(lambda b: wo_blk(b, y), lambda b: wo_blk(b, y).at[pl.ds(0, 16)],
                      lambda b: wo_blk(b, y).at[pl.ds(16, 32)])

    def round_y(block, low, high):
        st = {}
        sib = []

        def share(b):
            sib.append(post(block(c, b), block(c, b), sibling, landing=block(oc, b)))

        def begin():
            src = block(c, y)
            st["r"] = post(src, src, to_y(1), landing=block(c, yat(-1)))
            st["l"] = post(src, src, to_y(-1), landing=block(c, yat(1)))
            share(y)

        def middle():
            st["r"].arrived()
            st["rr"] = post(low(yat(-1)), low(yat(-1)), to_y(1), landing=low(yat(2)))
            st["l"].arrived()
            st["ll"] = post(high(yat(1)), high(yat(1)), to_y(-1), landing=high(yat(2)))
            share(yat(-1))
            share(yat(1))

        def end():
            st["rr"].arrived()
            st["ll"].arrived()
            share(yat(2))

        def ready():
            for link in sib:
                link.arrived()
        return begin, middle, end, ready

    def w_y(i):
        return round_y(lambda cc, b: wbuf.at[i, cc, :, b], lambda b: wbuf.at[i, c, pl.ds(0, 4), b],
                       lambda b: wbuf.at[i, c, pl.ds(4, 4), b])

    wo_rows = pl.ds(2 * c, 2)
    wo_begin, wo_middle, wo_end, wo_ready = round_y(
        lambda cc, b: wo.at[pl.ds(2 * cc, 2), :, b], lambda b: wo.at[wo_rows, pl.ds(0, 2), b],
        lambda b: wo.at[wo_rows, pl.ds(2, 2), b])
    q_begin, q_middle, q_end, q_ready = w_y(0)
    k_begin, k_middle, k_end, k_ready = w_y(1)

    in_kv.wait()
    wk_step(0)
    wv_y = [post(wbuf.at[2, c, z, y], wbuf.at[2, c, z, y], to_y(d), landing=wbuf.at[2, c, z, yat(-d)])
            for d in (1, 3, 2)]

    @pl.when(wo_self)
    def _():
        wo_local.wait()

    @pl.when(jnp.logical_not(wo_self))
    def _():
        wo_first(False).wait_send()
        wo_first(True).wait_recv()

    wo_step(0)

    rows_i = lax.broadcasted_iota(jnp.int32, (ROWS, HD), 0)
    lanes_i = lax.broadcasted_iota(jnp.int32, (ROWS, HD), 1)
    for s in range(16):
        limit = counts[s * NY + y]
        keep = jnp.logical_or(rows_i < limit, lanes_i > 0)
        mask[s] = jnp.where(keep, 0.0, NEG).astype(BF16)

    wk_step(1)
    wo_step(1)
    in_k.wait()
    in_v.wait()
    for link in wq_z:
        link.arrived()
    q_begin()
    kv_step(0)
    wk_step(2)
    wo_step(2)

    @pl.when(stays)
    def _():
        tok_local.wait()

    @pl.when(jnp.logical_not(stays))
    def _():
        tok_copy(0).wait()
        tok_copy(1).wait()

    for copy in small:
        copy.wait()

    def modulate(i, carry):
        r = pl.ds(pl.multiple_of(i * 16, 16), 16)
        t = tok[r, :].astype(F32)
        mean = jnp.mean(t, axis=1, keepdims=True)
        t = t - mean
        var = jnp.mean(t * t, axis=1, keepdims=True)
        t = t * lax.rsqrt(var + 1e-6)
        xmod[r, :] = (t * (1.0 + scale[...]) + shift[...]).astype(BF16)
        return carry

    lax.fori_loop(0, ROWS // 16, modulate, 0)
    wk_step(3)
    wo_step(3)
    q_middle()
    wk_step(4)
    kv_step(1)
    q_end()
    k_begin()
    q_ready()
    kv_step(2)

    def project(i):
        return jnp.dot(xmod[...], wbuf[i].reshape(D, HQ), preferred_element_type=F32)

    def head_norm(r):
        return r / jnp.sqrt(jnp.mean(r * r, axis=1, keepdims=True) + 1e-6)

    raw = project(0)
    for j in range(3):
        cols = slice(j * HD, (j + 1) * HD)
        qbuf[y, :, cols] = (head_norm(raw[:, cols]) * gain[...]).astype(BF16)
    q_links = {}
    for d in (1, 3, 2):
        q_links[d] = post(qbuf.at[y], qbuf.at[y], to_y(d), landing=qbuf.at[yat(-d)])
    ones = jnp.ones((768, HD), BF16)

    lane = lax.broadcasted_iota(jnp.int32, (ROWS, HD), 1)

    def absorb(j, zs, fresh_start):
        cols = pl.ds(pl.multiple_of(j * HD, HD), HD)
        q = jnp.concatenate([qbuf[y, :, cols], jnp.where(lane == 0, 1.0, 0.0).astype(BF16)], axis=1)
        places = [(cc, zz) for cc in range(2) for zz in zs]
        kb = jnp.concatenate(
            [jnp.concatenate([kv[0, cc, zz, :, cols], mask[cc * NZ + zz]], axis=1) for cc, zz in places],
            axis=0)
        s = lax.dot_general(q, kb, (((1,), (1,)), ((), ())), preferred_element_type=F32)
        top = s[:, :HD]
        for t in range(1, 6):
            top = jnp.maximum(top, s[:, t * HD:(t + 1) * HD])
        m = jnp.max(top, axis=1, keepdims=True)
        if not fresh_start:
            old = run_m[j][:, :1]
            m = jnp.maximum(m, old)
        w = jnp.exp2((s - m) * C2).astype(BF16)
        vb = jnp.concatenate([kv[1, cc, zz, :, cols] for cc, zz in places], axis=0)
        acc = jnp.dot(w, jnp.concatenate([vb, ones], axis=1), preferred_element_type=F32)
        if not fresh_start:
            acc = acc + run_acc[j] * jnp.exp2((old - m) * C2)
        run_m[j] = jnp.broadcast_to(m, (ROWS, HD))
        run_acc[j] = acc

    def absorb_all(zs, fresh_start):
        def one(j, carry):
            absorb(j, zs, fresh_start)
            return carry
        lax.fori_loop(0, 3, one, 0)

    others = (1, 3, 2)
    wide = len(others) * ROWS
    lane_w = lax.broadcasted_iota(jnp.int32, (wide, HD), 1)

    def remote_head(j):
        cols = slice(j * HD, (j + 1) * HD)
        q = jnp.concatenate([qbuf[yat(d), :, cols] for d in others], axis=0)
        q = jnp.concatenate([q, jnp.where(lane_w == 0, 1.0, 0.0).astype(BF16)], axis=1)

        def scores(b):
            cc, zz = b // 2, 4 * (b % 2)
            kb = jnp.concatenate([kv[0, cc, zz:zz + 4, :, cols].reshape(768, HD),
                                  mask[4 * b:4 * b + 4].reshape(768, HD)], axis=1)
            return lax.dot_general(q, kb, (((1,), (1,)), ((), ())), preferred_element_type=F32)

        m, acc, s = None, None, scores(0)
        for b in range(4):
            ahead = scores(b + 1) if b < 3 else None
            top = s[:, :HD]
            for t in range(1, 6):
                top = jnp.maximum(top, s[:, t * HD:(t + 1) * HD])
            new = jnp.max(top, axis=1, keepdims=True)
            if m is not None:
                new = jnp.maximum(new, m)
            w = jnp.exp2((s - new) * C2).astype(BF16)
            cc, zz = b // 2, 4 * (b % 2)
            vb = jnp.concatenate([kv[1, cc, zz:zz + 4, :, cols].reshape(768, HD), ones], axis=1)
            pv = jnp.dot(w, vb, preferred_element_type=F32)
            acc = pv if m is None else acc * jnp.exp2((m - new) * C2) + pv
            m, s = new, ahead
        total = acc[:, HD:]
        o = (acc[:, :HD] / total).astype(BF16)
        lse = m * C2 + jnp.log2(total)
        stat[...] = jnp.where(lane_w % 4 == j, lse, 0.0 if j == 0 else stat[...])
        for n, d in enumerate(others):
            osend[d, j] = o[n * ROWS:(n + 1) * ROWS]
            o_links.append(post(osend.at[d, j], orecv.at[d, j], to_y(d)))
        if j == 2:
            full = stat[...]
            top = full.astype(BF16).astype(F32)
            mid = (full - top).astype(BF16).astype(F32)
            low = full - top - mid
            packed = jnp.where(lane_w < 4, top, jnp.where(lane_w < 8, mid, low)).astype(BF16)
            for n, d in enumerate(others):
                osend[d, 3] = packed[n * ROWS:(n + 1) * ROWS]
                o_links.append(post(osend.at[d, 3], orecv.at[d, 3], to_y(d)))

    o_links = []
    kv_wait(1, 2)
    absorb_all((zat(-1), zat(1)), True)
    k_middle()
    wo_step(4)
    wo_begin()
    kv_wait(3, 4)
    absorb_all((zat(-2), zat(2)), False)
    kv_step(3)
    for link in wv_y:
        link.arrived()
    wv_step(0)
    kv_wait(5, 6)
    absorb_all((zat(-3), zat(3)), False)
    kv_step(4)
    wv_step(1)
    kv_wait(0, 7)
    for link in q_links.values():
        link.arrived()
    remote_head(0)
    k_end()
    wv_step(2)
    wo_middle()
    remote_head(1)
    wv_step(3)
    wo_end()
    remote_head(2)
    wv_step(4)
    k_ready()
    raw = project(1)
    for j in range(3):
        cols = slice(j * HD, (j + 1) * HD)
        mix[:, cols] = head_norm(raw[:, cols]).astype(BF16)
    for link in wv_sib:
        link.arrived()
    mix[:, HQ:] = project(2).astype(BF16)

    for link in key_state[0] + val_state[0] + (key_sib[0], val_sib[0]):
        link.done()
    kv[0, c, z] = mix[:, :HQ]
    kv[1, c, z] = mix[:, HQ:]

    att_links = []
    for j in range(3):
        cols = slice(j * HD, (j + 1) * HD)
        absorb(j, (z, zat(4)), False)
        if j == 0:
            for link in o_links:
                link.arrived()
        total = run_acc[j][:, HD:]
        parts = [run_acc[j][:, :HD] / total]
        lses = [run_m[j][:, :1] * C2 + jnp.log2(total[:, :1])]
        for d in (1, 3, 2):
            parts.append(orecv[d, j].astype(F32))
            st = jnp.where(jnp.logical_and(lane % 4 == j, lane < 12), orecv[d, 3].astype(F32), 0.0)
            lses.append(jnp.sum(st, axis=1, keepdims=True))
        top = functools.reduce(jnp.maximum, lses)
        ws = [jnp.exp2(v - top) for v in lses]
        total = functools.reduce(jnp.add, ws)
        mixd = functools.reduce(jnp.add, [w * o for w, o in zip(ws, parts)])
        att[x, :, cols] = (mixd / total).astype(BF16)
        for k in (1, 3, 2):
            att_links.append(post(att.at[x, :, pl.ds(j * HD, HD)], att.at[x, :, pl.ds(j * HD, HD)],
                                  dev(xat(k), z, y, c),
                                  landing=att.at[xat(-k), :, pl.ds(j * HD, HD)]))
    wo_ready()
    in_g.wait()
    for link in att_links:
        link.arrived()
    last = []
    for n in range(3):
        acc = jnp.zeros((ROWS, 256), F32)
        for g in range(NX):
            wt = wo[g].reshape(768, HQ)[n * 256:(n + 1) * 256]
            acc = acc + lax.dot_general(att[g], wt, (((1,), (1,)), ((), ())),
                                        preferred_element_type=F32)
        cols = slice(n * 256, (n + 1) * 256)
        mix[:, cols] = (acc * gbuf[cols].reshape(1, 256)).astype(BF16)
        part = pl.ds(n * 256, 256)
        last.append(Swap(mix.at[:, part], out.at[:, part], out.at[:, part]).start())
    for swap in last:
        swap.wait()
    for link in links:
        link.done()
    assert next_sem[0] <= N_SEM, next_sem[0]


def shards(tokens, valid_counts, mod_shift, mod_scale, mod_gate, q_gain, w_qkv, w_out,
           stale_keys, stale_values):
    hbm = pl.BlockSpec(memory_space=pltpu.HBM)
    return pl.pallas_call(
        kernel,
        out_shape=jax.ShapeDtypeStruct((ROWS, 768), BF16),
        in_specs=[pl.BlockSpec(memory_space=pltpu.SMEM)] + [hbm] * 9,
        out_specs=hbm,
        scratch_shapes=[
            pltpu.VMEM((ROWS, D), BF16),
            pltpu.VMEM((1, D), F32),
            pltpu.VMEM((1, D), F32),
            pltpu.VMEM((1, HD), F32),
            pltpu.VMEM((ROWS, D), BF16),
            pltpu.VMEM((3, 2, NZ, NY, SHARD, HQ), BF16),
            pltpu.VMEM((2, 2, NZ, ROWS, HQ), BF16),
            pltpu.VMEM((16, ROWS, HD), BF16),
            pltpu.VMEM((NY, ROWS, HQ), BF16),
            pltpu.VMEM((3 * ROWS, HD), F32),
            pltpu.VMEM((NY, 4, ROWS, HD), BF16),
            pltpu.VMEM((NY, 4, ROWS, HD), BF16),
            pltpu.VMEM((NX, ROWS, HQ), BF16),
            pltpu.VMEM((4, 4, NY, SHARD, HQ), BF16),
            pltpu.VMEM((768,), F32),
            pltpu.VMEM((ROWS, 768), BF16),
            pltpu.VMEM((3, ROWS, HD), F32),
            pltpu.VMEM((3, ROWS, 2 * HD), F32),
            pltpu.SemaphoreType.DMA((N_SEM,)),
            pltpu.SemaphoreType.DMA((N_SEM,)),
        ],
        compiler_params=pltpu.CompilerParams(
            collective_id=0, has_side_effects=True, vmem_limit_bytes=63 * 2**20),
    )(valid_counts, tokens, mod_scale.reshape(1, D), mod_shift.reshape(1, D),
      q_gain.reshape(1, HD), mod_gate, jnp.transpose(w_qkv, (1, 0, 2)),
      jnp.transpose(w_out), stale_keys, stale_values)


def solution(mesh):
    in_specs = (
        P("patch", None), P(), P(), P(), P("head"), P(), P("patch", None, "head"),
        P("head", "patch"), P("patch", "head"), P("patch", "head"),
    )
    return jax.shard_map(shards, mesh=mesh, in_specs=in_specs, out_specs=P("patch", "head"),
                         check_vma=False)
```

```python
import functools
import math

import jax
import jax.numpy as jnp
from jax import lax
from jax.experimental import pallas as pl
from jax.experimental.pallas import tpu as pltpu
from jax.sharding import PartitionSpec as P

MESH = pl.DeviceIdType.MESH
F32 = jnp.float32
BF16 = jnp.bfloat16
ROWS = 192
D = 3072
HQ = 384
HD = 128
NZ, NY, NX = 8, 4, 4
SHARD = 48
C2 = math.log2(math.e) / math.sqrt(HD)
NEG = -1e30
N_SEM = 168


def dev(x, z, y, c):
    return ((lax.rem(x, 2) * NZ + z) * NY + y, (x // 2) * 2 + c)


def kernel(counts, tokens, scale_in, shift_in, gain_in, gate, w_in, wo_in, k_in, v_in, out,
           tok, scale, shift, gain, xmod, wbuf, kv, mask, qbuf, stat, osend, orecv, att, wo, gbuf, mix,
           run_m, run_acc, ssem, rsem):
    p = lax.axis_index("patch")
    h = lax.axis_index("head")
    xl, z, y = p // (NZ * NY), lax.rem(p // NY, NZ), lax.rem(p, NY)
    xh, c = h // 2, lax.rem(h, 2)
    x = xh * 2 + xl
    oc = 1 - c

    def zat(k):
        return lax.rem(z + k + NZ, NZ)

    def yat(k):
        return lax.rem(y + k + NY, NY)

    def xat(k):
        return lax.rem(x + k + NX, NX)

    def to_z(k):
        return dev(x, zat(k), y, c)

    def to_y(k):
        return dev(x, z, yat(k), c)

    sibling = dev(x, z, y, oc)
    stays = c == xl

    next_sem = [0]

    def new_sem():
        next_sem[0] += 1
        return next_sem[0] - 1

    class Link:
        def __init__(self, src, dst, target, landing=None):
            n = new_sem()
            self.send = pltpu.make_async_remote_copy(
                src_ref=src, dst_ref=dst, send_sem=ssem.at[n], recv_sem=rsem.at[n],
                device_id=target, device_id_type=MESH)
            land = dst if landing is None else landing
            self.recv = pltpu.make_async_remote_copy(
                src_ref=land, dst_ref=land, send_sem=ssem.at[n], recv_sem=rsem.at[n],
                device_id=target, device_id_type=MESH)
            self.n = n
            self.sent = False

        def start(self):
            self.send.start()
            return self

        def arrived(self):
            self.recv.wait_recv()

        def done(self):
            if not self.sent:
                self.send.wait_send()
                self.sent = True

    links = []

    def post(src, dst, target, landing=None):
        link = Link(src, dst, target, landing).start()
        links.append(link)
        return link

    small = [pltpu.make_async_copy(a, b, ssem.at[new_sem()])
             for a, b in ((scale_in, scale), (shift_in, shift), (gain_in, gain))]
    for copy in small:
        copy.start()

    barrier = pltpu.get_barrier_semaphore()
    for k in range(NX):
        for cc in range(2):
            if k == 0 and cc == 0:
                continue
            pl.semaphore_signal(barrier, inc=1, device_id=dev(xat(k), z, y, lax.rem(c + cc, 2)),
                                device_id_type=MESH)
    for k in range(1, NZ):
        pl.semaphore_signal(barrier, inc=1, device_id=to_z(k), device_id_type=MESH)
    for k in range(1, NY):
        pl.semaphore_signal(barrier, inc=1, device_id=to_y(k), device_id_type=MESH)

    @pl.when(z // 4 != xl)
    def _():
        pl.semaphore_signal(barrier, inc=1, device_id=dev(2 * c + xh, zat(4), y, 1), device_id_type=MESH)

    rows_i = lax.broadcasted_iota(jnp.int32, (ROWS, HD), 0)
    lanes_i = lax.broadcasted_iota(jnp.int32, (ROWS, HD), 1)
    for s in range(16):
        limit = counts[s * NY + y]
        keep = jnp.logical_or(rows_i < limit, lanes_i > 0)
        mask[s] = jnp.where(keep, 0.0, NEG).astype(BF16)

    pl.semaphore_wait(barrier, 2 * NX - 1 + NZ - 1 + NY - 1 + c)

    partner = dev(xh * 2 + c, z, y, xl)

    class Swap:
        def __init__(self, src, here, there):
            n = new_sem()
            self.local = pltpu.make_async_copy(src, here, ssem.at[n])
            self.remote = pltpu.make_async_remote_copy(
                src_ref=src, dst_ref=there, send_sem=ssem.at[n], recv_sem=rsem.at[n],
                device_id=partner, device_id_type=MESH)
            self.landing = pltpu.make_async_remote_copy(
                src_ref=here, dst_ref=here, send_sem=ssem.at[n], recv_sem=rsem.at[n],
                device_id=partner, device_id_type=MESH)

        def start(self):
            @pl.when(stays)
            def _():
                self.local.start()

            @pl.when(jnp.logical_not(stays))
            def _():
                self.remote.start()
            return self

        def wait(self):
            @pl.when(stays)
            def _():
                self.local.wait()

            @pl.when(jnp.logical_not(stays))
            def _():
                self.remote.wait_send()
                self.landing.wait_recv()

    in_q = Swap(w_in.at[pl.ds(0, 1)], wbuf.at[pl.ds(0, 1), c, z, y], wbuf.at[pl.ds(0, 1), oc, z, y]).start()
    in_k = Swap(k_in, kv.at[0, c, z], kv.at[0, oc, z]).start()
    in_v = Swap(v_in, kv.at[1, c, z], kv.at[1, oc, z]).start()
    in_kv = Swap(w_in.at[pl.ds(1, 2)], wbuf.at[pl.ds(1, 2), c, z, y], wbuf.at[pl.ds(1, 2), oc, z, y]).start()

    wo_x, wo_c = 2 * xl + z // 4, xh
    wo_self = jnp.logical_and(jnp.logical_and(wo_x == x, wo_c == c), c == 0)
    wo_sem = new_sem()

    def wo_blk(zz, ys, cc=c):
        group = 2 * cc + jnp.where(zz // 4 == xl, 0, 1)
        return wo.at[group, lax.rem(zz, 4), ys]

    def wo_first(landing):
        dst = wo.at[h, lax.rem(z, 4), y]
        if landing:
            dst = wo_blk(z, y)
        return pltpu.make_async_remote_copy(
            src_ref=wo_in, dst_ref=dst, send_sem=ssem.at[wo_sem], recv_sem=rsem.at[wo_sem],
            device_id=dev(wo_x, lax.rem(z + 4 * c, NZ), y, wo_c), device_id_type=MESH)

    wo_local = pltpu.make_async_copy(wo_in, wo.at[h, lax.rem(z, 4), y], ssem.at[wo_sem])

    @pl.when(wo_self)
    def _():
        wo_local.start()

    @pl.when(jnp.logical_not(wo_self))
    def _():
        wo_first(False).start()

    tok_sem = [new_sem(), new_sem()]
    tok_local = pltpu.make_async_copy(tokens, tok, ssem.at[tok_sem[0]])

    def tok_copy(k):
        rows = pl.ds(0, 64) if k == 0 else pl.ds(64, 128)
        xo = x + 1 - 2 * xl if k == 0 else lax.rem(x + 3 + 2 * xl, NX)
        return pltpu.make_async_remote_copy(
            src_ref=tokens.at[rows], dst_ref=tok.at[rows], send_sem=ssem.at[tok_sem[k]],
            recv_sem=rsem.at[tok_sem[k]], device_id=dev(xo, z, y, oc), device_id_type=MESH)

    @pl.when(stays)
    def _():
        tok_local.start()

    @pl.when(jnp.logical_not(stays))
    def _():
        tok_copy(0).start()
        tok_copy(1).start()

    in_g = Swap(gate, gbuf, gbuf).start()

    in_q.wait()
    wq_z = []
    for k in (1, -1, 2, -2, 3, -3, 4):
        wq_z.append(post(wbuf.at[0, c, z, y], wbuf.at[0, c, z, y], to_z(k),
                         landing=wbuf.at[0, c, zat(-k), y]))

    def ring(block, first, second):
        state = {}

        def step(s):
            if s > 0:
                for link in state[s - 1]:
                    link.arrived()
            if s > 3:
                return
            if s < 3:
                right = post(block(zat(-s)), block(zat(-s)), to_z(1), landing=block(zat(-1 - s)))
                left = post(block(zat(s)), block(zat(s)), to_z(-1), landing=block(zat(1 + s)))
            else:
                right = post(first(zat(-s)), first(zat(-s)), to_z(1), landing=first(zat(-1 - s)))
                left = post(second(zat(s)), second(zat(s)), to_z(-1), landing=second(zat(1 + s)))
            state[s] = (right, left)
        return step, state

    def shared_ring(block, first, second):
        hop, state = ring(lambda b: block(b, c), first, second)
        shares = []

        def share(b):
            shares.append(post(block(b, c), block(b, c), sibling, landing=block(b, oc)))

        def step(s):
            hop(s)
            if s == 0:
                share(z)
            elif s < 4:
                share(zat(-s))
                share(zat(s))
            else:
                share(zat(4))
        return step, state, shares

    wk_step, _ = ring(lambda b: wbuf.at[1, c, b, y], lambda b: wbuf.at[1, c, b, y, pl.ds(0, 16)],
                      lambda b: wbuf.at[1, c, b, y, pl.ds(16, 32)])
    upper, lower = pl.ds(0, ROWS // 2), pl.ds(ROWS // 2, ROWS // 2)
    key_step, key_state, key_sib = shared_ring(
        lambda b, cc: kv.at[0, cc, b], lambda b: kv.at[0, c, b, upper], lambda b: kv.at[0, c, b, lower])
    val_step, val_state, val_sib = shared_ring(
        lambda b, cc: kv.at[1, cc, b], lambda b: kv.at[1, c, b, upper], lambda b: kv.at[1, c, b, lower])

    def kv_step(s):
        key_step(s)
        val_step(s)

    def kv_wait(*which):
        for i in which:
            key_sib[i].arrived()
            val_sib[i].arrived()

    lo_y, hi_y = pl.ds(0, 2), pl.ds(2, 2)
    wv_step, _, wv_sib = shared_ring(
        lambda b, cc: wbuf.at[2, cc, b], lambda b: wbuf.at[2, c, b, lo_y], lambda b: wbuf.at[2, c, b, hi_y])
    wo_step, _ = ring(lambda b: wo_blk(b, y), lambda b: wo_blk(b, y).at[pl.ds(0, 16)],
                      lambda b: wo_blk(b, y).at[pl.ds(16, 32)])

    def round_y(block, low, high):
        st = {}
        sib = []

        def share(b):
            sib.append(post(block(c, b), block(c, b), sibling, landing=block(oc, b)))

        def begin():
            src = block(c, y)
            st["r"] = post(src, src, to_y(1), landing=block(c, yat(-1)))
            st["l"] = post(src, src, to_y(-1), landing=block(c, yat(1)))
            share(y)

        def middle():
            st["r"].arrived()
            st["rr"] = post(low(yat(-1)), low(yat(-1)), to_y(1), landing=low(yat(2)))
            st["l"].arrived()
            st["ll"] = post(high(yat(1)), high(yat(1)), to_y(-1), landing=high(yat(2)))
            share(yat(-1))
            share(yat(1))

        def end():
            st["rr"].arrived()
            st["ll"].arrived()
            share(yat(2))

        def ready():
            for link in sib:
                link.arrived()
        return begin, middle, end, ready

    def w_y(i):
        return round_y(lambda cc, b: wbuf.at[i, cc, :, b], lambda b: wbuf.at[i, c, pl.ds(0, 4), b],
                       lambda b: wbuf.at[i, c, pl.ds(4, 4), b])

    wo_rows = pl.ds(2 * c, 2)
    wo_begin, wo_middle, wo_end, wo_ready = round_y(
        lambda cc, b: wo.at[pl.ds(2 * cc, 2), :, b], lambda b: wo.at[wo_rows, pl.ds(0, 2), b],
        lambda b: wo.at[wo_rows, pl.ds(2, 2), b])
    q_begin, q_middle, q_end, q_ready = w_y(0)
    k_begin, k_middle, k_end, k_ready = w_y(1)

    in_kv.wait()
    wk_step(0)
    wv_y = [post(wbuf.at[2, c, z, y], wbuf.at[2, c, z, y], to_y(d), landing=wbuf.at[2, c, z, yat(-d)])
            for d in (1, 3, 2)]

    @pl.when(wo_self)
    def _():
        wo_local.wait()

    @pl.when(jnp.logical_not(wo_self))
    def _():
        wo_first(False).wait_send()
        wo_first(True).wait_recv()

    wo_step(0)

    wk_step(1)
    wo_step(1)
    in_k.wait()
    in_v.wait()
    kv_step(0)
    for link in wq_z:
        link.arrived()
    q_begin()
    wk_step(2)
    wo_step(2)

    @pl.when(stays)
    def _():
        tok_local.wait()

    @pl.when(jnp.logical_not(stays))
    def _():
        tok_copy(0).wait()
        tok_copy(1).wait()

    for copy in small:
        copy.wait()

    def modulate(i, carry):
        r = pl.ds(pl.multiple_of(i * 16, 16), 16)
        t = tok[r, :].astype(F32)
        mean = jnp.mean(t, axis=1, keepdims=True)
        t = t - mean
        var = jnp.mean(t * t, axis=1, keepdims=True)
        t = t * lax.rsqrt(var + 1e-6)
        xmod[r, :] = (t * (1.0 + scale[...]) + shift[...]).astype(BF16)
        return carry

    lax.fori_loop(0, ROWS // 16, modulate, 0)
    wk_step(3)
    wo_step(3)
    q_middle()
    wk_step(4)
    kv_step(1)
    q_end()
    k_begin()
    q_ready()
    kv_step(2)

    def project(i):
        return jnp.dot(xmod[...], wbuf[i].reshape(D, HQ), preferred_element_type=F32)

    def head_norm(r):
        return r / jnp.sqrt(jnp.mean(r * r, axis=1, keepdims=True) + 1e-6)

    raw = project(0)
    for j in range(3):
        cols = slice(j * HD, (j + 1) * HD)
        qbuf[y, :, cols] = (head_norm(raw[:, cols]) * gain[...]).astype(BF16)
    q_links = {}
    for d in (1, 3, 2):
        q_links[d] = post(qbuf.at[y], qbuf.at[y], to_y(d), landing=qbuf.at[yat(-d)])
    ones = jnp.ones((768, HD), BF16)

    lane = lax.broadcasted_iota(jnp.int32, (ROWS, HD), 1)

    def absorb(j, zs, fresh_start):
        cols = pl.ds(pl.multiple_of(j * HD, HD), HD)
        q = jnp.concatenate([qbuf[y, :, cols], jnp.where(lane == 0, 1.0, 0.0).astype(BF16)], axis=1)
        places = [(cc, zz) for cc in range(2) for zz in zs]
        kb = jnp.concatenate(
            [jnp.concatenate([kv[0, cc, zz, :, cols], mask[cc * NZ + zz]], axis=1) for cc, zz in places],
            axis=0)
        s = lax.dot_general(q, kb, (((1,), (1,)), ((), ())), preferred_element_type=F32)
        top = s[:, :HD]
        for t in range(1, 6):
            top = jnp.maximum(top, s[:, t * HD:(t + 1) * HD])
        m = jnp.max(top, axis=1, keepdims=True)
        if not fresh_start:
            old = run_m[j][:, :1]
            m = jnp.maximum(m, old)
        w = jnp.exp2((s - m) * C2).astype(BF16)
        vb = jnp.concatenate([kv[1, cc, zz, :, cols] for cc, zz in places], axis=0)
        acc = jnp.dot(w, jnp.concatenate([vb, ones], axis=1), preferred_element_type=F32)
        if not fresh_start:
            acc = acc + run_acc[j] * jnp.exp2((old - m) * C2)
        run_m[j] = jnp.broadcast_to(m, (ROWS, HD))
        run_acc[j] = acc

    def absorb_all(zs, fresh_start):
        def one(j, carry):
            absorb(j, zs, fresh_start)
            return carry
        lax.fori_loop(0, 3, one, 0)

    others = (1, 3, 2)
    wide = len(others) * ROWS
    lane_w = lax.broadcasted_iota(jnp.int32, (wide, HD), 1)

    def remote_head(j):
        cols = slice(j * HD, (j + 1) * HD)
        q = jnp.concatenate([qbuf[yat(d), :, cols] for d in others], axis=0)
        q = jnp.concatenate([q, jnp.where(lane_w == 0, 1.0, 0.0).astype(BF16)], axis=1)

        def scores(b):
            cc, zz = b // 2, 4 * (b % 2)
            kb = jnp.concatenate([kv[0, cc, zz:zz + 4, :, cols].reshape(768, HD),
                                  mask[4 * b:4 * b + 4].reshape(768, HD)], axis=1)
            return lax.dot_general(q, kb, (((1,), (1,)), ((), ())), preferred_element_type=F32)

        m, acc, s = None, None, scores(0)
        for b in range(4):
            ahead = scores(b + 1) if b < 3 else None
            top = s[:, :HD]
            for t in range(1, 6):
                top = jnp.maximum(top, s[:, t * HD:(t + 1) * HD])
            new = jnp.max(top, axis=1, keepdims=True)
            if m is not None:
                new = jnp.maximum(new, m)
            w = jnp.exp2((s - new) * C2).astype(BF16)
            cc, zz = b // 2, 4 * (b % 2)
            vb = jnp.concatenate([kv[1, cc, zz:zz + 4, :, cols].reshape(768, HD), ones], axis=1)
            pv = jnp.dot(w, vb, preferred_element_type=F32)
            acc = pv if m is None else acc * jnp.exp2((m - new) * C2) + pv
            m, s = new, ahead
        total = acc[:, HD:]
        o = (acc[:, :HD] / total).astype(BF16)
        lse = m * C2 + jnp.log2(total)
        stat[...] = jnp.where(lane_w % 4 == j, lse, 0.0 if j == 0 else stat[...])
        for n, d in enumerate(others):
            osend[d, j] = o[n * ROWS:(n + 1) * ROWS]
            o_links.append(post(osend.at[d, j], orecv.at[d, j], to_y(d)))
        if j == 2:
            full = stat[...]
            top = full.astype(BF16).astype(F32)
            mid = (full - top).astype(BF16).astype(F32)
            low = full - top - mid
            packed = jnp.where(lane_w < 4, top, jnp.where(lane_w < 8, mid, low)).astype(BF16)
            for n, d in enumerate(others):
                osend[d, 3] = packed[n * ROWS:(n + 1) * ROWS]
                o_links.append(post(osend.at[d, 3], orecv.at[d, 3], to_y(d)))

    o_links = []
    kv_wait(1, 2)
    absorb_all((zat(-1), zat(1)), True)
    k_middle()
    wo_step(4)
    wo_begin()
    kv_wait(3, 4)
    absorb_all((zat(-2), zat(2)), False)
    kv_step(3)
    for link in wv_y:
        link.arrived()
    wv_step(0)
    kv_wait(5, 6)
    absorb_all((zat(-3), zat(3)), False)
    kv_step(4)
    wv_step(1)
    kv_wait(0, 7)
    for link in q_links.values():
        link.arrived()
    remote_head(0)
    k_end()
    wv_step(2)
    wo_middle()
    remote_head(1)
    wv_step(3)
    wo_end()
    remote_head(2)
    wv_step(4)
    k_ready()
    raw = project(1)
    for j in range(3):
        cols = slice(j * HD, (j + 1) * HD)
        mix[:, cols] = head_norm(raw[:, cols]).astype(BF16)
    for link in wv_sib:
        link.arrived()
    mix[:, HQ:] = project(2).astype(BF16)

    for link in key_state[0] + val_state[0] + (key_sib[0], val_sib[0]):
        link.done()
    kv[0, c, z] = mix[:, :HQ]
    kv[1, c, z] = mix[:, HQ:]

    att_links = []
    for j in range(3):
        cols = slice(j * HD, (j + 1) * HD)
        absorb(j, (z, zat(4)), False)
        if j == 0:
            for link in o_links:
                link.arrived()
        total = run_acc[j][:, HD:]
        parts = [run_acc[j][:, :HD] / total]
        lses = [run_m[j][:, :1] * C2 + jnp.log2(total[:, :1])]
        for d in (1, 3, 2):
            parts.append(orecv[d, j].astype(F32))
            st = jnp.where(jnp.logical_and(lane % 4 == j, lane < 12), orecv[d, 3].astype(F32), 0.0)
            lses.append(jnp.sum(st, axis=1, keepdims=True))
        top = functools.reduce(jnp.maximum, lses)
        ws = [jnp.exp2(v - top) for v in lses]
        total = functools.reduce(jnp.add, ws)
        mixd = functools.reduce(jnp.add, [w * o for w, o in zip(ws, parts)])
        att[x, :, cols] = (mixd / total).astype(BF16)
        for k in (1, 3, 2):
            att_links.append(post(att.at[x, :, pl.ds(j * HD, HD)], att.at[x, :, pl.ds(j * HD, HD)],
                                  dev(xat(k), z, y, c),
                                  landing=att.at[xat(-k), :, pl.ds(j * HD, HD)]))
    wo_ready()
    in_g.wait()
    for link in att_links:
        link.arrived()
    last = []
    for n in range(3):
        acc = jnp.zeros((ROWS, 256), F32)
        for g in range(NX):
            wt = wo[g].reshape(768, HQ)[n * 256:(n + 1) * 256]
            acc = acc + lax.dot_general(att[g], wt, (((1,), (1,)), ((), ())),
                                        preferred_element_type=F32)
        cols = slice(n * 256, (n + 1) * 256)
        mix[:, cols] = (acc * gbuf[cols].reshape(1, 256)).astype(BF16)
        part = pl.ds(n * 256, 256)
        last.append(Swap(mix.at[:, part], out.at[:, part], out.at[:, part]).start())
    for swap in last:
        swap.wait()
    for link in links:
        link.done()
    assert next_sem[0] <= N_SEM, next_sem[0]


def shards(tokens, valid_counts, mod_shift, mod_scale, mod_gate, q_gain, w_qkv, w_out,
           stale_keys, stale_values):
    hbm = pl.BlockSpec(memory_space=pltpu.HBM)
    return pl.pallas_call(
        kernel,
        out_shape=jax.ShapeDtypeStruct((ROWS, 768), BF16),
        in_specs=[pl.BlockSpec(memory_space=pltpu.SMEM)] + [hbm] * 9,
        out_specs=hbm,
        scratch_shapes=[
            pltpu.VMEM((ROWS, D), BF16),
            pltpu.VMEM((1, D), F32),
            pltpu.VMEM((1, D), F32),
            pltpu.VMEM((1, HD), F32),
            pltpu.VMEM((ROWS, D), BF16),
            pltpu.VMEM((3, 2, NZ, NY, SHARD, HQ), BF16),
            pltpu.VMEM((2, 2, NZ, ROWS, HQ), BF16),
            pltpu.VMEM((16, ROWS, HD), BF16),
            pltpu.VMEM((NY, ROWS, HQ), BF16),
            pltpu.VMEM((3 * ROWS, HD), F32),
            pltpu.VMEM((NY, 4, ROWS, HD), BF16),
            pltpu.VMEM((NY, 4, ROWS, HD), BF16),
            pltpu.VMEM((NX, ROWS, HQ), BF16),
            pltpu.VMEM((4, 4, NY, SHARD, HQ), BF16),
            pltpu.VMEM((768,), F32),
            pltpu.VMEM((ROWS, 768), BF16),
            pltpu.VMEM((3, ROWS, HD), F32),
            pltpu.VMEM((3, ROWS, 2 * HD), F32),
            pltpu.SemaphoreType.DMA((N_SEM,)),
            pltpu.SemaphoreType.DMA((N_SEM,)),
        ],
        compiler_params=pltpu.CompilerParams(
            collective_id=0, has_side_effects=True, vmem_limit_bytes=63 * 2**20),
    )(valid_counts, tokens, mod_scale.reshape(1, D), mod_shift.reshape(1, D),
      q_gain.reshape(1, HD), mod_gate, jnp.transpose(w_qkv, (1, 0, 2)),
      jnp.transpose(w_out), stale_keys, stale_values)


def solution(mesh):
    in_specs = (
        P("patch", None), P(), P(), P(), P("head"), P(), P("patch", None, "head"),
        P("head", "patch"), P("patch", "head"), P("patch", "head"),
    )
    return jax.shard_map(shards, mesh=mesh, in_specs=in_specs, out_specs=P("patch", "head"),
                         check_vma=False)
```
